32 devices in a mesh: row: 4 (over z), col: 4 (over y, x), pan: 2 (over core).
Axes of the slice: x: 2, y: 2, z: 4, core: 2. Of those that a mesh axis runs over, the one named last changes fastest.
Arguments:
- plan_values: bfloat16 [4096, 32, 256], P('row', 'col', 'pan'), may hold values from 0.099609375 to 1
- plan_blocks: int32 [4, 32], P('row', 'col'), may hold values from 0 to 31, as said below
- first_values: bfloat16 [16, 3, 256, 256], P('row'), may hold values from -0.21875 to 0.21875
- first_blocks: int32 [16, 3], P('row'), may hold values from 0 to 3, as said below
- second_values: bfloat16 [32, 6, 256, 256], P('col', None, None, 'pan'), may hold values from -0.15625 to 0.15625
- second_blocks: int32 [32, 6], P('col'), may hold values from 0 to 7, as said below
- weight_first: float32 [4096], P('row'), may hold values from 0.5 to 2
- weight_second: float32 [32, 256], P('col', 'pan'), may hold values from 0.5 to 2
- offset_first: float32 [4096], P('row'), may hold values from -3 to 3
- offset_second: float32 [32, 256], P('col', 'pan'), may hold values from -3 to 3
Outputs:
- new_plan: bfloat16 [4096, 32, 256], P('row', 'col', 'pan')
- scale_first: float32 [4096], P('row')
- scale_second: float32 [32, 256], P('col', 'pan')
The draws below stay inside these ranges and needn't reach their ends.
Inputs may be any that keep to these rules, and one draw needn't show every extreme that they name: `plan_blocks`: each entry is a slice-B block number; its column panel is the entry // 8. Within the 8 slots of one index of col (aligned groups of the second dimension) no column panel is named more than 2 times, and in every row panel one column panel is named exactly 2 times by every such group. `first_blocks`: block numbers within the row panel of the slice-A block; the 3 entries of a row are distinct. `second_blocks`: block numbers within the column panel of the slice-B block; the 6 entries of a row are distinct.
All inputs are finite; a program needn't handle non-finite values.
Results may differ from the reference program's by a relative error of at most 0.0087.
Values may be sent and summed in bfloat16 or wider, within the bound.
A program may use at most 128 MiB of HBM per device.

```python
import math
import jax
import jax.numpy as jnp

BLOCK = 256
PANEL_BLOCKS = 4
COL_BLOCKS = 8
FIRST_NEAR = 3
SECOND_NEAR = 6
PLAN_SLOTS = 8
CAP = 2
PANELS = 4
COL_PANELS = 4
PANEL_ROWS = 1024
ROW_BLOCKS_A = 16
ROWS_A = 4096
BLOCKS_B = 32
PLAN_WIDTH = 32


def draw_plan_blocks(key, part):
    folded = jax.random.fold_in(key, 7)
    subkeys = jax.random.split(folded, 4)
    hot_panel = jax.random.randint(subkeys[0], (PANELS, 1, 1), 0, COL_PANELS)
    spare_panels = COL_PANELS - 1
    scores = jax.random.randint(subkeys[1], (PANELS, COL_PANELS, spare_panels), 0, 1 << 20) * spare_panels + jnp.arange(spare_panels, dtype=jnp.int32)[None, None, :]
    ordering = jnp.argsort(scores, axis=-1).astype(jnp.int32)
    spare_slots = PLAN_SLOTS - CAP
    chosen = ordering[:, :, jnp.arange(spare_slots, dtype=jnp.int32) % spare_panels]
    far_panel = (hot_panel + 1 + chosen) % COL_PANELS
    near_panel = jnp.broadcast_to(hot_panel, (PANELS, COL_PANELS, CAP))
    panels_drawn = jnp.concatenate([near_panel, far_panel], axis=-1)
    shuffle_scores = jax.random.randint(subkeys[2], (PANELS, COL_PANELS, PLAN_SLOTS), 0, 1 << 20) * PLAN_SLOTS + jnp.arange(PLAN_SLOTS, dtype=jnp.int32)[None, None, :]
    shuffle = jnp.argsort(shuffle_scores, axis=-1).astype(jnp.int32)
    panels_drawn = jnp.take_along_axis(panels_drawn, shuffle, axis=-1)
    inside = jax.random.randint(subkeys[3], (PANELS, COL_PANELS, PLAN_SLOTS), 0, COL_BLOCKS)
    return (panels_drawn * COL_BLOCKS + inside).reshape(PANELS, COL_PANELS * PLAN_SLOTS).astype(jnp.int32)


def distinct_rows(key, row_count, choices_count, taken):
    scores = jax.random.randint(key, (row_count, choices_count), 0, 1 << 20) * choices_count + jnp.arange(choices_count, dtype=jnp.int32)[None, :]
    ordering = jnp.argsort(scores, axis=-1).astype(jnp.int32)
    return ordering[:, :taken].astype(jnp.int32)


def draw_first_blocks(key, part):
    return distinct_rows(jax.random.fold_in(key, 11), ROW_BLOCKS_A, PANEL_BLOCKS, FIRST_NEAR)


def draw_second_blocks(key, part):
    return distinct_rows(jax.random.fold_in(key, 13), BLOCKS_B, COL_BLOCKS, SECOND_NEAR)


def block_scale(key, extent, cuts, smallest, largest):
    level, own = 1.0, jax.random.fold_in(key, 6)
    for axis_at, parts in cuts:
        steps = jnp.exp(jax.random.uniform(jax.random.fold_in(own, axis_at), (parts,), jnp.float32, smallest / len(cuts), largest / len(cuts)))
        level = level * jnp.repeat(steps, extent[axis_at] // parts).reshape([-1 if axis == axis_at else 1 for axis in range(len(extent))])
    return level


def noise(rng, shape, scale, most, cuts=(), kind=jnp.bfloat16):
    result = scale * jax.random.normal(rng, shape, jnp.float32)
    if cuts:
        result = result * block_scale(rng, shape, cuts, -0.22, 0.18)
    return jnp.clip(result, -most, most).astype(kind)


def setup_inputs(seed: int = 0) -> dict:
    key_list = jax.random.split(jax.random.key(seed), 11)
    return {
        "plan_values": jnp.clip(jnp.exp(math.log(1.0) - 2.306499 * jax.random.uniform(key_list[0], (ROWS_A, PLAN_WIDTH, BLOCK), jnp.float32) ** block_scale(key_list[0], (ROWS_A, PLAN_WIDTH, BLOCK), ((0, 4), (1, 4), (2, 2)), -0.2, 0.2)), 0.099609375, 1.0).astype(jnp.bfloat16),
        "plan_blocks": draw_plan_blocks(jax.random.fold_in(key_list[10], 71), 0),
        "first_values": noise(key_list[2], (ROW_BLOCKS_A, FIRST_NEAR, BLOCK, BLOCK), (BLOCK * FIRST_NEAR) ** -0.5, 0.21875, ((0, 4),)),
        "first_blocks": draw_first_blocks(jax.random.fold_in(key_list[10], 71), 0),
        "second_values": noise(key_list[4], (BLOCKS_B, SECOND_NEAR, BLOCK, BLOCK), (BLOCK * SECOND_NEAR) ** -0.5, 0.15625, ((0, 4), (3, 2))),
        "second_blocks": draw_second_blocks(jax.random.fold_in(key_list[10], 71), 0),
        "weight_first": jnp.clip(jnp.exp(math.log(2.0) - 1.3862944 * jax.random.uniform(key_list[6], (ROWS_A,), jnp.float32) ** block_scale(key_list[6], (ROWS_A,), ((0, 4),), -0.2, 0.2)), 0.5, 2.0),
        "weight_second": jnp.clip(jnp.exp(math.log(2.0) - 1.3862944 * jax.random.uniform(key_list[7], (BLOCKS_B, BLOCK), jnp.float32) ** block_scale(key_list[7], (BLOCKS_B, BLOCK), ((0, 4), (1, 2)), -0.2, 0.2)), 0.5, 2.0),
        "offset_first": noise(key_list[8], (ROWS_A,), 0.5, 3.0, ((0, 4),), jnp.float32),
        "offset_second": noise(key_list[9], (BLOCKS_B, BLOCK), 0.5, 3.0, ((0, 4), (1, 2)), jnp.float32),
    }


def reference(plan_values, plan_blocks, first_values, first_blocks, second_values, second_blocks, weight_first, weight_second, offset_first, offset_second):
    panel_rows = PANEL_ROWS
    plan_width = PLAN_WIDTH * BLOCK
    panel_base = (jnp.arange(BLOCKS_B, dtype=jnp.int32) // COL_BLOCKS) * COL_BLOCKS
    kept_blocks = []
    row_scales = []
    colsum = jnp.zeros((BLOCKS_B, BLOCK), jnp.float32)
    counts = jnp.zeros((BLOCKS_B,), jnp.float32)
    for panel_index in range(PANELS):
        row_start = panel_index * panel_rows
        row_tiles = plan_values[row_start:row_start + panel_rows].reshape(PANEL_BLOCKS, BLOCK, plan_width)
        near_list = first_blocks[panel_index * PANEL_BLOCKS:(panel_index + 1) * PANEL_BLOCKS].astype(jnp.int32)
        coefficients = first_values[panel_index * PANEL_BLOCKS:(panel_index + 1) * PANEL_BLOCKS]
        running = jnp.zeros((PANEL_BLOCKS, BLOCK, plan_width), jnp.float32)
        for neighbor in range(FIRST_NEAR):
            picked = row_tiles[near_list[:, neighbor]].astype(jnp.float32)
            running = running + jnp.einsum("iab,ibn->ian", coefficients[:, neighbor].astype(jnp.float32), picked)
        product = running.astype(jnp.bfloat16).reshape(panel_rows, PLAN_WIDTH, BLOCK)
        named_blocks = plan_blocks[panel_index].astype(jnp.int32)
        dense_plan = jnp.zeros((panel_rows, BLOCKS_B, BLOCK), jnp.float32).at[:, named_blocks].add(product.astype(jnp.float32)).astype(jnp.bfloat16)
        present = jnp.minimum(jnp.zeros((BLOCKS_B,), jnp.float32).at[named_blocks].add(jnp.float32(1.0)), jnp.float32(1.0))
        crossed = jnp.zeros((panel_rows, BLOCKS_B, BLOCK), jnp.float32)
        dense_wide = dense_plan.astype(jnp.float32)
        for neighbor in range(SECOND_NEAR):
            partial_sum = jnp.einsum("rkb,kbc->rkc", dense_wide, second_values[:, neighbor].astype(jnp.float32))
            targets = (panel_base + second_blocks[:, neighbor].astype(jnp.int32)).astype(jnp.int32)
            crossed = crossed.at[:, targets].add(partial_sum)
        kernel = present[None, :, None] * jnp.exp(crossed - offset_first[row_start:row_start + panel_rows][:, None, None] - offset_second[None])
        totals = jnp.sum(kernel, axis=(1, 2))
        row_scale = weight_first[row_start:row_start + panel_rows] * jnp.float32(plan_width) / totals
        weighted = kernel * row_scale[:, None, None]
        colsum = colsum + jnp.sum(weighted, axis=0)
        counts = counts + present * jnp.float32(panel_rows)
        kept_blocks.append(weighted[:, named_blocks, :])
        row_scales.append(row_scale)
    scale_second = weight_second * counts[:, None] / jnp.where(counts[:, None] > 0, colsum, jnp.float32(1.0))
    pieces = []
    for panel_index in range(PANELS):
        named_blocks = plan_blocks[panel_index].astype(jnp.int32)
        pieces.append((kept_blocks[panel_index] * scale_second[named_blocks][None]).astype(jnp.bfloat16))
    new_plan = jnp.concatenate(pieces, axis=0)
    scale_first = jnp.concatenate(row_scales, axis=0)
    return (new_plan, scale_first, scale_second)
```

```python
import functools

import jax
import jax.numpy as jnp
from jax import lax
from jax.experimental import pallas as pl
from jax.experimental.pallas import tpu as pltpu
from jax.sharding import PartitionSpec as P

CAP = 2
PAN = 2
GROUP = 8
MESH = pl.DeviceIdType.MESH
BF16_MAX = float(jnp.finfo(jnp.bfloat16).max)


def ranked_slot(read, slots, blocks_here, panel, rank):
    seen, found = jnp.int32(0), jnp.int32(-1)
    for s in range(slots):
        match = (lax.div(read(s), jnp.int32(blocks_here)) == panel).astype(jnp.int32)
        hit = match * (seen == rank).astype(jnp.int32)
        found = jnp.where(hit > 0, jnp.int32(s), found)
        seen = seen + match
    return found


def kernel(
    dims,
    tm_hbm,
    names_smem,
    names_vmem,
    first_hbm,
    near_smem,
    second_hbm,
    near_second_smem,
    weight_first,
    weight_second,
    offset_first,
    offset_second,
    out_ref,
    scale_first_ref,
    scale_second_ref,
    tm,
    first,
    second,
    product,
    outgoing,
    arrived,
    values,
    home,
    row_sums,
    col_sums,
    scales,
    names,
    row_scale,
    names_all,
    second_index,
    slot_of,
    label_of,
    present_of,
    item_of,
    local_sem,
    name_send,
    name_recv,
    out_send,
    out_recv,
    pan_send,
    pan_recv,
    back_send,
    back_recv,
    sum_send,
    sum_recv,
    col_send,
    col_recv,
    scale_send,
    scale_recv,
):
    C, R_AXIS, tiles, block, slots, half, blocks_here, near1, near2 = dims
    rows_total = tiles * block
    items = C * CAP
    row, me, pan = lax.axis_index("row"), lax.axis_index("col"), lax.axis_index("pan")
    other = 1 - pan

    def ahead(o):
        return lax.rem(me + o, C)

    def behind(o):
        return lax.rem(me - o + C, C)

    def row_ahead(o):
        return lax.rem(row + o, R_AXIS)

    def row_behind(o):
        return lax.rem(row - o + R_AXIS, R_AXIS)

    load_tm = pltpu.make_async_copy(tm_hbm, tm, local_sem.at[0])
    load_first = pltpu.make_async_copy(first_hbm, first, local_sem.at[1])
    load_second = pltpu.make_async_copy(
        second_hbm, second.at[pl.ds(0, blocks_here * near2)], local_sem.at[2]
    )
    load_tm.start()
    load_first.start()
    load_second.start()

    barrier = pltpu.get_barrier_semaphore()
    for oc in range(C):
        for oh in range(PAN):
            if oc or oh:
                pl.semaphore_signal(
                    barrier,
                    inc=1,
                    device_id=(row, ahead(oc), other if oh else pan),
                    device_id_type=MESH,
                )
    for o in range(1, R_AXIS):
        pl.semaphore_signal(
            barrier, inc=1, device_id=(row_ahead(o), me, pan), device_id_type=MESH
        )

    names[me] = jnp.zeros((8, 128), jnp.int32)
    names[me, 0:1, 0:slots] = names_vmem[...]
    second[blocks_here * near2] = jnp.zeros((block, half), jnp.bfloat16)
    row_sums[me * PAN + pan] = jnp.zeros((row_sums.shape[1], block), jnp.float32)

    def own_name(s):
        return names_smem[0, s]

    for d in range(C):
        for rank in range(CAP):
            slot_of[d * CAP + rank] = ranked_slot(own_name, slots, blocks_here, d, rank)
    for s in range(slots):
        panel = lax.div(own_name(s), jnp.int32(blocks_here))
        rank = jnp.int32(0)
        for t in range(s):
            rank = rank + (lax.div(own_name(t), jnp.int32(blocks_here)) == panel).astype(jnp.int32)
        item_of[0, s] = panel
        item_of[1, s] = jnp.minimum(rank, CAP - 1)
        item_of[2, s] = lax.rem(own_name(s), jnp.int32(blocks_here))

    pl.semaphore_wait(barrier, C * PAN - 1 + R_AXIS - 1)

    def send_names(o):
        return pltpu.make_async_remote_copy(
            src_ref=names.at[me],
            dst_ref=names.at[me],
            send_sem=name_send.at[o],
            recv_sem=name_recv.at[o],
            device_id=(row, ahead(o), pan),
            device_id_type=MESH,
        )

    def take_names(o):
        src = behind(o)
        return pltpu.make_async_remote_copy(
            src_ref=names.at[src],
            dst_ref=names.at[src],
            send_sem=name_send.at[o],
            recv_sem=name_recv.at[o],
            device_id=(row, src, pan),
            device_id_type=MESH,
        )

    for o in range(1, C):
        send_names(o).start()

    def dispatch(i, o):
        return pltpu.make_async_remote_copy(
            src_ref=outgoing.at[i, ahead(o)],
            dst_ref=arrived.at[pan, i, me],
            send_sem=out_send.at[i, o],
            recv_sem=out_recv.at[i, o],
            device_id=(row, ahead(o), pan),
            device_id_type=MESH,
        )

    def arrival(i, o):
        return pltpu.make_async_remote_copy(
            src_ref=outgoing.at[i, behind(o)],
            dst_ref=arrived.at[pan, i, behind(o)],
            send_sem=out_send.at[i, o],
            recv_sem=out_recv.at[i, o],
            device_id=(row, behind(o), pan),
            device_id_type=MESH,
        )

    def share(i, o):
        return pltpu.make_async_remote_copy(
            src_ref=arrived.at[pan, i, behind(o)],
            dst_ref=arrived.at[pan, i, behind(o)],
            send_sem=pan_send.at[i, o],
            recv_sem=pan_recv.at[i, o],
            device_id=(row, me, other),
            device_id_type=MESH,
        )

    def shared(i, o):
        return pltpu.make_async_remote_copy(
            src_ref=arrived.at[other, i, behind(o)],
            dst_ref=arrived.at[other, i, behind(o)],
            send_sem=pan_send.at[i, o],
            recv_sem=pan_recv.at[i, o],
            device_id=(row, me, other),
            device_id_type=MESH,
        )

    def give_back(i, o):
        return pltpu.make_async_remote_copy(
            src_ref=outgoing.at[i, ahead(o)],
            dst_ref=home.at[i, me],
            send_sem=back_send.at[i, o],
            recv_sem=back_recv.at[i, o],
            device_id=(row, ahead(o), pan),
            device_id_type=MESH,
        )

    def got_back(i, o):
        return pltpu.make_async_remote_copy(
            src_ref=outgoing.at[i, behind(o)],
            dst_ref=home.at[i, behind(o)],
            send_sem=back_send.at[i, o],
            recv_sem=back_recv.at[i, o],
            device_id=(row, behind(o), pan),
            device_id_type=MESH,
        )

    load_tm.wait()
    load_first.wait()

    def first_step(i, carry):
        left = jnp.concatenate([first[i, q] for q in range(near1)], axis=1)
        step = 2 * half
        for n in range(slots * half // step):
            right = jnp.concatenate(
                [tm[near_smem[i, q], :, n * step : (n + 1) * step] for q in range(near1)], axis=0
            )
            piece = jnp.dot(left, right, preferred_element_type=jnp.float32).astype(jnp.bfloat16)
            product[2 * n] = piece[:, :half]
            product[2 * n + 1] = piece[:, half:]
        for o in list(range(1, C)) + [0]:
            d = ahead(o)
            for rank in range(CAP):
                slot = slot_of[d * CAP + rank]
                piece = product[jnp.maximum(slot, 0)]
                keep = (slot >= 0).astype(jnp.float32).astype(jnp.bfloat16)
                piece = piece if items == slots else piece * keep
                if o:
                    outgoing[i, d, rank] = piece
                else:
                    arrived[pan, i, me, rank] = piece
            if o:
                dispatch(i, o).start()
            else:
                share(i, 0).start()
        return carry

    lax.fori_loop(0, tiles, first_step, 0)

    for o in range(1, C):
        take_names(o).wait_recv()
    copy_names = pltpu.make_async_copy(names, names_all, local_sem.at[3])
    copy_names.start()
    copy_names.wait()
    for src in range(C):
        for rank in range(CAP):
            read = lambda s: names_all[src, 0, s]
            slot = ranked_slot(read, slots, blocks_here, me, rank)
            name = lax.rem(read(jnp.maximum(slot, 0)), jnp.int32(blocks_here))
            label_of[src * CAP + rank] = jnp.where(slot >= 0, name, jnp.int32(-1))
    for l in range(blocks_here):
        hits = jnp.int32(0)
        for t in range(items):
            hits = hits + (label_of[t] == l).astype(jnp.int32)
        present_of[l] = jnp.minimum(hits, 1)

    def index_step(k, carry):
        for l in range(blocks_here):
            found = jnp.int32(blocks_here * near2)
            for q in range(near2):
                found = jnp.where(near_second_smem[k, q] == l, k * near2 + q, found)
            second_index[k, l] = found
        return carry

    lax.fori_loop(0, blocks_here, index_step, 0)
    load_second.wait()

    def spread(line):
        return jnp.transpose(jnp.broadcast_to(line, (half, block)))

    def second_step(i, carry):
        for o in range(1, C):
            arrival(i, o).wait_recv()
            share(i, o).start()
        for o in range(C):
            shared(i, o).wait_recv()
        at = pl.ds(pl.multiple_of(i * block, block), block)
        first_offset = spread(offset_first[pl.ds(i, 1), :])
        labels = [jnp.maximum(label_of[t], 0) for t in range(items)]
        total = jnp.zeros((block, half), jnp.float32)
        for pair in range(blocks_here // 2):
            crossed = None
            for start in range(0, items, GROUP):
                group = range(start, min(start + GROUP, items))
                left = jnp.concatenate(
                    [arrived[p, i, t // CAP, t % CAP] for t in group for p in range(PAN)], axis=1
                )
                right = jnp.concatenate(
                    [
                        jnp.concatenate(
                            [second[second_index[labels[t], 2 * pair + e]] for e in range(2)],
                            axis=1,
                        )
                        for t in group
                    ],
                    axis=0,
                )
                part = jnp.dot(left, right, preferred_element_type=jnp.float32)
                crossed = part if crossed is None else crossed + part
            for e in range(2):
                l = 2 * pair + e
                here = crossed[:, e * half : (e + 1) * half]
                seen = present_of[l].astype(jnp.float32)
                value = seen * jnp.exp(here - first_offset - offset_second[l : l + 1, :])
                values[l, at, :] = value
                total = total + value
        row_sums[me * PAN + pan, pl.ds(i, 1), :] = jnp.sum(
            jnp.transpose(total), axis=0, keepdims=True
        )
        for o in range(1, C):
            dispatch(i, o).wait_send()
        for o in list(range(1, C)) + [0]:
            d = ahead(o)
            for rank in range(CAP):
                label = jnp.maximum(label_of[d * CAP + rank], 0)
                value = jnp.minimum(values[label, at, :], BF16_MAX).astype(jnp.bfloat16)
                if o:
                    outgoing[i, d, rank] = value
                else:
                    home[i, me, rank] = value
            if o:
                give_back(i, o).start()
        return carry

    lax.fori_loop(0, tiles, second_step, 0)

    def sums_out(oc, oh):
        mine = me * PAN + pan
        return pltpu.make_async_remote_copy(
            src_ref=row_sums.at[mine],
            dst_ref=row_sums.at[mine],
            send_sem=sum_send.at[oc * PAN + oh],
            recv_sem=sum_recv.at[oc * PAN + oh],
            device_id=(row, ahead(oc), other if oh else pan),
            device_id_type=MESH,
        )

    def sums_in(oc, oh):
        theirs = behind(oc) * PAN + (other if oh else pan)
        return pltpu.make_async_remote_copy(
            src_ref=row_sums.at[theirs],
            dst_ref=row_sums.at[theirs],
            send_sem=sum_send.at[oc * PAN + oh],
            recv_sem=sum_recv.at[oc * PAN + oh],
            device_id=(row, behind(oc), other if oh else pan),
            device_id_type=MESH,
        )

    peers = [(oc, oh) for oc in range(C) for oh in range(PAN) if oc or oh]
    for oc, oh in peers:
        sums_out(oc, oh).start()
    for oc, oh in peers:
        sums_in(oc, oh).wait_recv()
    totals = row_sums[0, 0:tiles, :]
    for t in range(1, C * PAN):
        totals = totals + row_sums[t, 0:tiles, :]
    width = float(slots * C * block)
    scale_first_ref[...] = weight_first[...] * width / totals

    def col_step(i, sums):
        at = pl.ds(pl.multiple_of(i * block, block), block)
        scale = spread(scale_first_ref[pl.ds(i, 1), :])
        row_scale[at, :] = scale
        return tuple(
            sums[l] + jnp.sum(values[l, at, :] * scale, axis=0, keepdims=True)
            for l in range(blocks_here)
        )

    sums = lax.fori_loop(
        0, tiles, col_step, tuple(jnp.zeros((1, half), jnp.float32) for _ in range(blocks_here))
    )
    for l in range(blocks_here):
        col_sums[row, l : l + 1, :] = sums[l]
        col_sums[row, blocks_here + l : blocks_here + l + 1, :] = jnp.full(
            (1, half), present_of[l].astype(jnp.float32) * float(rows_total), jnp.float32
        )

    def cols_out(o):
        return pltpu.make_async_remote_copy(
            src_ref=col_sums.at[row],
            dst_ref=col_sums.at[row],
            send_sem=col_send.at[o],
            recv_sem=col_recv.at[o],
            device_id=(row_ahead(o), me, pan),
            device_id_type=MESH,
        )

    def cols_in(o):
        return pltpu.make_async_remote_copy(
            src_ref=col_sums.at[row_behind(o)],
            dst_ref=col_sums.at[row_behind(o)],
            send_sem=col_send.at[o],
            recv_sem=col_recv.at[o],
            device_id=(row_behind(o), me, pan),
            device_id_type=MESH,
        )

    for o in range(1, R_AXIS):
        cols_out(o).start()
    for o in range(1, R_AXIS):
        cols_in(o).wait_recv()
    both = col_sums[0]
    for t in range(1, R_AXIS):
        both = both + col_sums[t]
    colsum, counts = both[:blocks_here], both[blocks_here:]
    scale_second = weight_second[...] * counts / jnp.where(counts > 0, colsum, 1.0)
    scale_second_ref[...] = scale_second
    scales[me] = scale_second

    def scale_out(o):
        return pltpu.make_async_remote_copy(
            src_ref=scales.at[me],
            dst_ref=scales.at[me],
            send_sem=scale_send.at[o],
            recv_sem=scale_recv.at[o],
            device_id=(row, ahead(o), pan),
            device_id_type=MESH,
        )

    def scale_in(o):
        return pltpu.make_async_remote_copy(
            src_ref=scales.at[behind(o)],
            dst_ref=scales.at[behind(o)],
            send_sem=scale_send.at[o],
            recv_sem=scale_recv.at[o],
            device_id=(row, behind(o), pan),
            device_id_type=MESH,
        )

    for o in range(1, C):
        scale_out(o).start()
    for o in range(1, C):
        scale_in(o).wait_recv()

    def finish_waits(i, carry):
        for o in range(1, C):
            got_back(i, o).wait_recv()
        return carry

    lax.fori_loop(0, tiles, finish_waits, 0)

    def last_step(i, carry):
        at = pl.ds(pl.multiple_of(i * block, block), block)
        scale = row_scale[at, :]
        for s in range(slots):
            panel, rank, name = item_of[0, s], item_of[1, s], item_of[2, s]
            value = home[i, panel, rank].astype(jnp.float32) * scale
            value = value * scales[panel, pl.ds(name, 1), :]
            out_ref[at, s * half : (s + 1) * half] = value.astype(jnp.bfloat16)
        return carry

    lax.fori_loop(0, tiles, last_step, 0)

    def drain(i, carry):
        for o in range(C):
            share(i, o).wait_send()
        for o in range(1, C):
            give_back(i, o).wait_send()
        return carry

    lax.fori_loop(0, tiles, drain, 0)
    for o in range(1, C):
        send_names(o).wait_send()
        scale_out(o).wait_send()
    for oc, oh in peers:
        sums_out(oc, oh).wait_send()
    for o in range(1, R_AXIS):
        cols_out(o).wait_send()


def local(
    plan_values,
    plan_blocks,
    first_values,
    first_blocks,
    second_values,
    second_blocks,
    weight_first,
    weight_second,
    offset_first,
    offset_second,
):
    C, R_AXIS = lax.axis_size("col"), lax.axis_size("row")
    rows, slots, half = plan_values.shape
    tiles, near1, block, _ = first_values.shape
    blocks_here, near2 = second_blocks.shape
    dims = (C, R_AXIS, tiles, block, slots, half, blocks_here, near1, near2)
    sum_rows = -(-tiles // 8) * 8
    bf16, f32, i32 = jnp.bfloat16, jnp.float32, jnp.int32
    vmem, smem = pltpu.VMEM, pltpu.SMEM
    dma = pltpu.SemaphoreType.DMA
    in_vmem, in_smem = pl.BlockSpec(memory_space=vmem), pl.BlockSpec(memory_space=smem)
    anywhere = pl.BlockSpec(memory_space=pl.ANY)
    out, scale_first, scale_second = pl.pallas_call(
        functools.partial(kernel, dims),
        out_shape=(
            jax.ShapeDtypeStruct((rows, slots * half), bf16),
            jax.ShapeDtypeStruct((tiles, block), f32),
            jax.ShapeDtypeStruct((blocks_here, half), f32),
        ),
        in_specs=[
            anywhere,
            in_smem,
            in_vmem,
            anywhere,
            in_smem,
            anywhere,
            in_smem,
            in_vmem,
            in_vmem,
            in_vmem,
            in_vmem,
        ],
        out_specs=(in_vmem, in_vmem, in_vmem),
        scratch_shapes=[
            vmem((tiles, block, slots * half), bf16),
            vmem((tiles, near1, block, block), bf16),
            vmem((blocks_here * near2 + 1, block, half), bf16),
            vmem((slots, block, half), bf16),
            vmem((tiles, C, CAP, block, half), bf16),
            vmem((PAN, tiles, C, CAP, block, half), bf16),
            vmem((blocks_here, rows, half), f32),
            vmem((tiles, C, CAP, block, half), bf16),
            vmem((C * PAN, sum_rows, block), f32),
            vmem((R_AXIS, 2 * blocks_here, half), f32),
            vmem((C, blocks_here, half), f32),
            vmem((C, 8, 128), i32),
            vmem((rows, half), f32),
            smem((C, 8, 128), i32),
            smem((blocks_here, blocks_here), i32),
            smem((C * CAP,), i32),
            smem((C * CAP,), i32),
            smem((blocks_here,), i32),
            smem((3, slots), i32),
            dma((4,)),
            dma((C,)),
            dma((C,)),
            dma((tiles, C)),
            dma((tiles, C)),
            dma((tiles, C)),
            dma((tiles, C)),
            dma((tiles, C)),
            dma((tiles, C)),
            dma((C * PAN,)),
            dma((C * PAN,)),
            dma((R_AXIS,)),
            dma((R_AXIS,)),
            dma((C,)),
            dma((C,)),
        ],
        compiler_params=pltpu.CompilerParams(
            collective_id=0, has_side_effects=True, vmem_limit_bytes=60 * 1024 * 1024
        ),
        name="gromov_step",
    )(
        plan_values.reshape(tiles, block, slots * half),
        plan_blocks,
        plan_blocks,
        first_values,
        first_blocks,
        second_values.reshape(blocks_here * near2, block, half),
        second_blocks,
        weight_first.reshape(tiles, block),
        weight_second,
        offset_first.reshape(tiles, block),
        offset_second,
    )
    return out.reshape(rows, slots, half), scale_first.reshape(rows), scale_second


def solution(mesh):
    return jax.shard_map(
        local,
        mesh=mesh,
        in_specs=(
            P("row", "col", "pan"),
            P("row", "col"),
            P("row", None, None, None),
            P("row", None),
            P("col", None, None, "pan"),
            P("col", None),
            P("row"),
            P("col", "pan"),
            P("row"),
            P("col", "pan"),
        ),
        out_specs=(P("row", "col", "pan"), P("row"), P("col", "pan")),
        check_vma=False,
    )
```

```python
import functools

import jax
import jax.numpy as jnp
from jax import lax
from jax.experimental import pallas as pl
from jax.experimental.pallas import tpu as pltpu
from jax.sharding import PartitionSpec as P

CAP = 2
PAN = 2
GROUP = 8
MESH = pl.DeviceIdType.MESH
BF16_MAX = float(jnp.finfo(jnp.bfloat16).max)


def ranked_slot(read, slots, blocks_here, panel, rank):
    seen, found = jnp.int32(0), jnp.int32(-1)
    for s in range(slots):
        match = (lax.div(read(s), jnp.int32(blocks_here)) == panel).astype(jnp.int32)
        hit = match * (seen == rank).astype(jnp.int32)
        found = jnp.where(hit > 0, jnp.int32(s), found)
        seen = seen + match
    return found


def kernel(
    dims,
    plan_hbm,
    names_smem,
    names_vmem,
    first_hbm,
    near_smem,
    second_hbm,
    near_second_smem,
    weight_first,
    weight_second,
    offset_first,
    offset_second,
    out_ref,
    scale_first_ref,
    scale_second_ref,
    plan,
    wide,
    tm,
    first,
    second,
    product,
    outgoing,
    arrived,
    values,
    finished,
    row_sums,
    col_sums,
    scales,
    names,
    row_scale,
    names_all,
    second_index,
    slot_of,
    label_of,
    present_of,
    item_of,
    local_sem,
    name_send,
    name_recv,
    out_send,
    out_recv,
    pan_send,
    pan_recv,
    back_send,
    back_recv,
    sum_send,
    sum_recv,
    col_send,
    col_recv,
    scale_send,
    scale_recv,
    plan_sem,
    done_sem,
    *home,
):
    C, R_AXIS, tiles, block, slots, half, blocks_here, near1, near2 = dims
    rows_total = tiles * block
    items = C * CAP
    row, me, pan = lax.axis_index("row"), lax.axis_index("col"), lax.axis_index("pan")
    other = 1 - pan

    def ahead(o):
        return lax.rem(me + o, C)

    def behind(o):
        return lax.rem(me - o + C, C)

    def row_ahead(o):
        return lax.rem(row + o, R_AXIS)

    def row_behind(o):
        return lax.rem(row - o + R_AXIS, R_AXIS)

    def load_plan(i):
        return pltpu.make_async_copy(
            plan_hbm.at[pl.ds(i * block, block)], plan.at[i], plan_sem.at[i]
        )

    load_first = pltpu.make_async_copy(first_hbm, first, local_sem.at[1])
    load_second = pltpu.make_async_copy(
        second_hbm, second.at[pl.ds(0, blocks_here * near2)], local_sem.at[2]
    )
    for i in range(tiles):
        load_plan(i).start()
    load_first.start()
    load_second.start()

    barrier = pltpu.get_barrier_semaphore()
    for oc in range(C):
        for oh in range(PAN):
            if oc or oh:
                pl.semaphore_signal(
                    barrier,
                    inc=1,
                    device_id=(row, ahead(oc), other if oh else pan),
                    device_id_type=MESH,
                )
    for o in range(1, R_AXIS):
        pl.semaphore_signal(
            barrier, inc=1, device_id=(row_ahead(o), me, pan), device_id_type=MESH
        )

    names[me] = jnp.zeros((8, 128), jnp.int32)
    names[me, 0:1, 0:slots] = names_vmem[...]
    second[blocks_here * near2] = jnp.zeros((block, half), jnp.bfloat16)

    def own_name(s):
        return names_smem[0, s]

    for d in range(C):
        for rank in range(CAP):
            slot_of[d * CAP + rank] = ranked_slot(own_name, slots, blocks_here, d, rank)
    for s in range(slots):
        panel = lax.div(own_name(s), jnp.int32(blocks_here))
        rank = jnp.int32(0)
        for t in range(s):
            rank = rank + (lax.div(own_name(t), jnp.int32(blocks_here)) == panel).astype(jnp.int32)
        item_of[0, s] = panel
        item_of[1, s] = jnp.minimum(rank, CAP - 1)
        item_of[2, s] = lax.rem(own_name(s), jnp.int32(blocks_here))

    def relayout(i, carry):
        load_plan(i).wait()
        wide[...] = plan[i].astype(jnp.float32).reshape(block * slots, half)
        for s in range(slots):
            lane = wide[pl.ds(s, block, stride=slots), :]
            tm[i, :, s * half : (s + 1) * half] = lane.astype(jnp.bfloat16)
        return carry

    lax.fori_loop(0, tiles, relayout, 0)

    pl.semaphore_wait(barrier, C * PAN - 1 + R_AXIS - 1)

    def send_names(o):
        return pltpu.make_async_remote_copy(
            src_ref=names.at[me],
            dst_ref=names.at[me],
            send_sem=name_send.at[o],
            recv_sem=name_recv.at[o],
            device_id=(row, ahead(o), pan),
            device_id_type=MESH,
        )

    def take_names(o):
        src = behind(o)
        return pltpu.make_async_remote_copy(
            src_ref=names.at[src],
            dst_ref=names.at[src],
            send_sem=name_send.at[o],
            recv_sem=name_recv.at[o],
            device_id=(row, src, pan),
            device_id_type=MESH,
        )

    for o in range(1, C):
        send_names(o).start()

    def dispatch(i, o):
        return pltpu.make_async_remote_copy(
            src_ref=outgoing.at[i, ahead(o)],
            dst_ref=arrived.at[pan, i, me],
            send_sem=out_send.at[i, o],
            recv_sem=out_recv.at[i, o],
            device_id=(row, ahead(o), pan),
            device_id_type=MESH,
        )

    def arrival(i, o):
        return pltpu.make_async_remote_copy(
            src_ref=outgoing.at[i, behind(o)],
            dst_ref=arrived.at[pan, i, behind(o)],
            send_sem=out_send.at[i, o],
            recv_sem=out_recv.at[i, o],
            device_id=(row, behind(o), pan),
            device_id_type=MESH,
        )

    def share(i, o):
        return pltpu.make_async_remote_copy(
            src_ref=arrived.at[pan, i, behind(o)],
            dst_ref=arrived.at[pan, i, behind(o)],
            send_sem=pan_send.at[i, o],
            recv_sem=pan_recv.at[i, o],
            device_id=(row, me, other),
            device_id_type=MESH,
        )

    def shared(i, o):
        return pltpu.make_async_remote_copy(
            src_ref=arrived.at[other, i, behind(o)],
            dst_ref=arrived.at[other, i, behind(o)],
            send_sem=pan_send.at[i, o],
            recv_sem=pan_recv.at[i, o],
            device_id=(row, me, other),
            device_id_type=MESH,
        )

    def give_back(i, o):
        return pltpu.make_async_remote_copy(
            src_ref=outgoing.at[i, ahead(o)],
            dst_ref=home[i].at[me],
            send_sem=back_send.at[i, o],
            recv_sem=back_recv.at[i, o],
            device_id=(row, ahead(o), pan),
            device_id_type=MESH,
        )

    def got_back(i, o):
        return pltpu.make_async_remote_copy(
            src_ref=outgoing.at[i, behind(o)],
            dst_ref=home[i].at[behind(o)],
            send_sem=back_send.at[i, o],
            recv_sem=back_recv.at[i, o],
            device_id=(row, behind(o), pan),
            device_id_type=MESH,
        )

    load_first.wait()

    def first_step(i, carry):
        left = jnp.concatenate([first[i, q] for q in range(near1)], axis=1)
        step = 2 * half
        for n in range(slots * half // step):
            right = jnp.concatenate(
                [tm[near_smem[i, q], :, n * step : (n + 1) * step] for q in range(near1)], axis=0
            )
            piece = jnp.dot(left, right, preferred_element_type=jnp.float32).astype(jnp.bfloat16)
            product[2 * n] = piece[:, :half]
            product[2 * n + 1] = piece[:, half:]
        for o in list(range(1, C)) + [0]:
            d = ahead(o)
            for rank in range(CAP):
                slot = slot_of[d * CAP + rank]
                piece = product[jnp.maximum(slot, 0)]
                keep = (slot >= 0).astype(jnp.float32).astype(jnp.bfloat16)
                piece = piece if items == slots else piece * keep
                if o:
                    outgoing[i, d, rank] = piece
                else:
                    arrived[pan, i, me, rank] = piece
            if o:
                dispatch(i, o).start()
            else:
                share(i, 0).start()
        return carry

    lax.fori_loop(0, tiles, first_step, 0)

    for o in range(1, C):
        take_names(o).wait_recv()
    copy_names = pltpu.make_async_copy(names, names_all, local_sem.at[3])
    copy_names.start()
    copy_names.wait()
    for src in range(C):
        for rank in range(CAP):
            read = lambda s: names_all[src, 0, s]
            slot = ranked_slot(read, slots, blocks_here, me, rank)
            name = lax.rem(read(jnp.maximum(slot, 0)), jnp.int32(blocks_here))
            label_of[src * CAP + rank] = jnp.where(slot >= 0, name, jnp.int32(-1))
    for l in range(blocks_here):
        hits = jnp.int32(0)
        for t in range(items):
            hits = hits + (label_of[t] == l).astype(jnp.int32)
        present_of[l] = jnp.minimum(hits, 1)

    def index_step(k, carry):
        for l in range(blocks_here):
            found = jnp.int32(blocks_here * near2)
            for q in range(near2):
                found = jnp.where(near_second_smem[k, q] == l, k * near2 + q, found)
            second_index[k, l] = found
        return carry

    lax.fori_loop(0, blocks_here, index_step, 0)
    load_second.wait()

    def spread(line):
        return jnp.transpose(jnp.broadcast_to(line, (half, block)))

    def sums_out(i, oc, oh):
        mine = me * PAN + pan
        return pltpu.make_async_remote_copy(
            src_ref=row_sums.at[mine, i],
            dst_ref=row_sums.at[mine, i],
            send_sem=sum_send.at[i, oc * PAN + oh],
            recv_sem=sum_recv.at[i, oc * PAN + oh],
            device_id=(row, ahead(oc), other if oh else pan),
            device_id_type=MESH,
        )

    def sums_in(i, oc, oh):
        theirs = behind(oc) * PAN + (other if oh else pan)
        return pltpu.make_async_remote_copy(
            src_ref=row_sums.at[theirs, i],
            dst_ref=row_sums.at[theirs, i],
            send_sem=sum_send.at[i, oc * PAN + oh],
            recv_sem=sum_recv.at[i, oc * PAN + oh],
            device_id=(row, behind(oc), other if oh else pan),
            device_id_type=MESH,
        )

    peers = [(oc, oh) for oc in range(C) for oh in range(PAN) if oc or oh]

    def send_home(i):
        for o in range(1, C):
            give_back(i, o).start()

    def second_step(i, carry, last=False):
        for o in range(1, C):
            arrival(i, o).wait_recv()
            share(i, o).start()
        if last:
            send_home(0)
        for o in range(C):
            shared(i, o).wait_recv()
        at = pl.ds(pl.multiple_of(i * block, block), block)
        first_offset = spread(offset_first[:, at])
        labels = [jnp.maximum(label_of[t], 0) for t in range(items)]
        total = jnp.zeros((block, half), jnp.float32)
        for pair in range(blocks_here // 2):
            crossed = None
            for start in range(0, items, GROUP):
                group = range(start, min(start + GROUP, items))
                left = jnp.concatenate(
                    [arrived[p, i, t // CAP, t % CAP] for t in group for p in range(PAN)], axis=1
                )
                right = jnp.concatenate(
                    [
                        jnp.concatenate(
                            [second[second_index[labels[t], 2 * pair + e]] for e in range(2)],
                            axis=1,
                        )
                        for t in group
                    ],
                    axis=0,
                )
                part = jnp.dot(left, right, preferred_element_type=jnp.float32)
                crossed = part if crossed is None else crossed + part
            for e in range(2):
                l = 2 * pair + e
                here = crossed[:, e * half : (e + 1) * half]
                seen = present_of[l].astype(jnp.float32)
                value = seen * jnp.exp(here - first_offset - offset_second[l : l + 1, :])
                values[l, at, :] = value
                total = total + value
        row_sums[me * PAN + pan, i] = jnp.sum(jnp.transpose(total), axis=0, keepdims=True)
        for oc, oh in peers:
            sums_out(i, oc, oh).start()
        for o in range(1, C):
            dispatch(i, o).wait_send()
        for d in range(C):
            for rank in range(CAP):
                label = jnp.maximum(label_of[d * CAP + rank], 0)
                value = jnp.minimum(values[label, at, :], BF16_MAX).astype(jnp.bfloat16)
                outgoing[i, d, rank] = value
        return carry

    lax.fori_loop(0, tiles - 1, second_step, 0)
    second_step(tiles - 1, 0, last=True)
    held = list(range(1, tiles))

    def release():
        if held:
            send_home(held.pop(0))

    release()
    for i in range(tiles):
        for oc, oh in peers:
            sums_in(i, oc, oh).wait_recv()
    width = float(slots * C * block)
    for i in range(tiles):
        part = slice(i * block, (i + 1) * block)
        totals = row_sums[0, i]
        for t in range(1, C * PAN):
            totals = totals + row_sums[t, i]
        scale_first_ref[:, part] = weight_first[:, part] * width / totals

    def col_step(i, sums):
        at = pl.ds(pl.multiple_of(i * block, block), block)
        scale = spread(scale_first_ref[:, at])
        row_scale[at, :] = scale
        return tuple(
            sums[l] + jnp.sum(values[l, at, :] * scale, axis=0, keepdims=True)
            for l in range(blocks_here)
        )

    sums = lax.fori_loop(
        0, tiles, col_step, tuple(jnp.zeros((1, half), jnp.float32) for _ in range(blocks_here))
    )
    for l in range(blocks_here):
        col_sums[row, l : l + 1, :] = sums[l]
        col_sums[row, blocks_here + l : blocks_here + l + 1, :] = jnp.full(
            (1, half), present_of[l].astype(jnp.float32) * float(rows_total), jnp.float32
        )

    def cols_out(o):
        return pltpu.make_async_remote_copy(
            src_ref=col_sums.at[row],
            dst_ref=col_sums.at[row],
            send_sem=col_send.at[o],
            recv_sem=col_recv.at[o],
            device_id=(row_ahead(o), me, pan),
            device_id_type=MESH,
        )

    def cols_in(o):
        return pltpu.make_async_remote_copy(
            src_ref=col_sums.at[row_behind(o)],
            dst_ref=col_sums.at[row_behind(o)],
            send_sem=col_send.at[o],
            recv_sem=col_recv.at[o],
            device_id=(row_behind(o), me, pan),
            device_id_type=MESH,
        )

    for o in range(1, R_AXIS):
        cols_out(o).start()
    release()
    for i in range(tiles):
        home[i][me] = outgoing[i, me]
    for o in range(1, R_AXIS):
        cols_in(o).wait_recv()
    both = col_sums[0]
    for t in range(1, R_AXIS):
        both = both + col_sums[t]
    colsum, counts = both[:blocks_here], both[blocks_here:]
    scale_second = weight_second[...] * counts / jnp.where(counts > 0, colsum, 1.0)
    scale_second_ref[...] = scale_second
    scales[me] = scale_second

    def scale_out(o):
        return pltpu.make_async_remote_copy(
            src_ref=scales.at[me],
            dst_ref=scales.at[me],
            send_sem=scale_send.at[o],
            recv_sem=scale_recv.at[o],
            device_id=(row, ahead(o), pan),
            device_id_type=MESH,
        )

    def scale_in(o):
        return pltpu.make_async_remote_copy(
            src_ref=scales.at[behind(o)],
            dst_ref=scales.at[behind(o)],
            send_sem=scale_send.at[o],
            recv_sem=scale_recv.at[o],
            device_id=(row, behind(o), pan),
            device_id_type=MESH,
        )

    for o in range(1, C):
        scale_out(o).start()
    while held:
        release()
    for o in range(1, C):
        scale_in(o).wait_recv()

    def store(i):
        return pltpu.make_async_copy(
            finished.at[i], out_ref.at[pl.ds(i * block, block)], done_sem.at[i]
        )

    for i in range(tiles):
        for o in range(1, C):
            got_back(i, o).wait_recv()
        scale = row_scale[i * block : (i + 1) * block, :]
        for s in range(slots):
            panel, rank, name = item_of[0, s], item_of[1, s], item_of[2, s]
            value = home[i][panel, rank].astype(jnp.float32) * scale
            value = value * scales[panel, pl.ds(name, 1), :]
            wide[pl.ds(s, block, stride=slots), :] = value
        finished[i] = wide[...].reshape(block, slots, half).astype(jnp.bfloat16)
        store(i).start()

    def drain(i, carry):
        for o in range(C):
            share(i, o).wait_send()
        for oc, oh in peers:
            sums_out(i, oc, oh).wait_send()
        return carry

    lax.fori_loop(0, tiles, drain, 0)
    for i in range(tiles):
        for o in range(1, C):
            give_back(i, o).wait_send()
    for o in range(1, C):
        send_names(o).wait_send()
        scale_out(o).wait_send()
    for o in range(1, R_AXIS):
        cols_out(o).wait_send()
    for i in range(tiles):
        store(i).wait()


def local(
    plan_values,
    plan_blocks,
    first_values,
    first_blocks,
    second_values,
    second_blocks,
    weight_first,
    weight_second,
    offset_first,
    offset_second,
):
    C, R_AXIS = lax.axis_size("col"), lax.axis_size("row")
    rows, slots, half = plan_values.shape
    tiles, near1, block, _ = first_values.shape
    blocks_here, near2 = second_blocks.shape
    dims = (C, R_AXIS, tiles, block, slots, half, blocks_here, near1, near2)
    bf16, f32, i32 = jnp.bfloat16, jnp.float32, jnp.int32
    vmem, smem = pltpu.VMEM, pltpu.SMEM
    dma = pltpu.SemaphoreType.DMA
    in_vmem, in_smem = pl.BlockSpec(memory_space=vmem), pl.BlockSpec(memory_space=smem)
    anywhere = pl.BlockSpec(memory_space=pl.ANY)
    out, scale_first, scale_second = pl.pallas_call(
        functools.partial(kernel, dims),
        out_shape=(
            jax.ShapeDtypeStruct((rows, slots, half), bf16),
            jax.ShapeDtypeStruct((1, rows), f32),
            jax.ShapeDtypeStruct((blocks_here, half), f32),
        ),
        in_specs=[
            anywhere,
            in_smem,
            in_vmem,
            anywhere,
            in_smem,
            anywhere,
            in_smem,
            in_vmem,
            in_vmem,
            in_vmem,
            in_vmem,
        ],
        out_specs=(anywhere, in_vmem, in_vmem),
        scratch_shapes=[
            vmem((tiles, block, slots, half), bf16),
            vmem((block * slots, half), f32),
            vmem((tiles, block, slots * half), bf16),
            vmem((tiles, near1, block, block), bf16),
            vmem((blocks_here * near2 + 1, block, half), bf16),
            vmem((slots, block, half), bf16),
            vmem((tiles, C, CAP, block, half), bf16),
            vmem((PAN, tiles, C, CAP, block, half), bf16),
            vmem((blocks_here, rows, half), f32),
            vmem((tiles, block, slots, half), bf16),
            vmem((C * PAN, tiles, 1, block), f32),
            vmem((R_AXIS, 2 * blocks_here, half), f32),
            vmem((C, blocks_here, half), f32),
            vmem((C, 8, 128), i32),
            vmem((rows, half), f32),
            smem((C, 8, 128), i32),
            smem((blocks_here, blocks_here), i32),
            smem((C * CAP,), i32),
            smem((C * CAP,), i32),
            smem((blocks_here,), i32),
            smem((3, slots), i32),
            dma((4,)),
            dma((C,)),
            dma((C,)),
            dma((tiles, C)),
            dma((tiles, C)),
            dma((tiles, C)),
            dma((tiles, C)),
            dma((tiles, C)),
            dma((tiles, C)),
            dma((tiles, C * PAN)),
            dma((tiles, C * PAN)),
            dma((R_AXIS,)),
            dma((R_AXIS,)),
            dma((C,)),
            dma((C,)),
            dma((tiles,)),
            dma((tiles,)),
        ]
        + [vmem((C, CAP, block, half), bf16)] * tiles,
        compiler_params=pltpu.CompilerParams(
            collective_id=0, has_side_effects=True, vmem_limit_bytes=60 * 1024 * 1024
        ),
        name="gromov_step",
    )(
        plan_values,
        plan_blocks,
        plan_blocks,
        first_values,
        first_blocks,
        second_values.reshape(blocks_here * near2, block, half),
        second_blocks,
        weight_first.reshape(1, rows),
        weight_second,
        offset_first.reshape(1, rows),
        offset_second,
    )
    return out, scale_first.reshape(rows), scale_second


def solution(mesh):
    return jax.shard_map(
        local,
        mesh=mesh,
        in_specs=(
            P("row", "col", "pan"),
            P("row", "col"),
            P("row", None, None, None),
            P("row", None),
            P("col", None, None, "pan"),
            P("col", None),
            P("row"),
            P("col", "pan"),
            P("row"),
            P("col", "pan"),
        ),
        out_specs=(P("row", "col", "pan"), P("row"), P("col", "pan")),
        check_vma=False,
    )
```

```python
import functools

import jax
import jax.numpy as jnp
from jax import lax
from jax.experimental import pallas as pl
from jax.experimental.pallas import tpu as pltpu
from jax.sharding import PartitionSpec as P

CAP = 2
PAN = 2
GROUP = 8
MESH = pl.DeviceIdType.MESH
BF16_MAX = float(jnp.finfo(jnp.bfloat16).max)


def ranked_slot(read, slots, blocks_here, panel, rank):
    seen, found = jnp.int32(0), jnp.int32(-1)
    for s in range(slots):
        match = (lax.div(read(s), jnp.int32(blocks_here)) == panel).astype(jnp.int32)
        hit = match * (seen == rank).astype(jnp.int32)
        found = jnp.where(hit > 0, jnp.int32(s), found)
        seen = seen + match
    return found


def kernel(
    dims,
    plan_hbm,
    names_smem,
    names_vmem,
    first_hbm,
    near_smem,
    second_hbm,
    near_second_smem,
    weight_first,
    weight_second,
    offset_first,
    offset_second,
    out_ref,
    scale_first_ref,
    scale_second_ref,
    plan,
    wide,
    tm,
    first,
    second,
    product,
    outgoing,
    arrived,
    values,
    finished,
    row_sums,
    col_sums,
    scales,
    names,
    row_scale,
    names_all,
    second_index,
    slot_of,
    label_of,
    present_of,
    item_of,
    local_sem,
    name_send,
    name_recv,
    out_send,
    out_recv,
    pan_send,
    pan_recv,
    back_send,
    back_recv,
    sum_send,
    sum_recv,
    col_send,
    col_recv,
    scale_send,
    scale_recv,
    plan_sem,
    done_sem,
    *home,
):
    C, R_AXIS, tiles, block, slots, half, blocks_here, near1, near2 = dims
    rows_total = tiles * block
    items = C * CAP
    row, me, pan = lax.axis_index("row"), lax.axis_index("col"), lax.axis_index("pan")
    other = 1 - pan

    bits = C.bit_length() - 1
    paired = C == 1 << bits

    def across(o):
        shift = o
        if bits > 1 and o % 4 in (1, 2):
            shift = o + pan * (1 if o % 4 == 1 else -1)
        result = 0
        for b in range(bits):
            result = result + lax.rem(lax.div(me, 1 << b) + lax.div(shift, 1 << b), 2) * (1 << b)
        return result

    def ahead(o):
        if o == 0:
            return me
        return across(o) if paired else lax.rem(me + o, C)

    def behind(o):
        if o == 0:
            return me
        return across(o) if paired else lax.rem(me - o + C, C)

    def row_ahead(o):
        return lax.rem(row + o, R_AXIS)

    def row_behind(o):
        return lax.rem(row - o + R_AXIS, R_AXIS)

    def load_plan(i):
        return pltpu.make_async_copy(
            plan_hbm.at[pl.ds(i * block, block)], plan.at[i], plan_sem.at[i]
        )

    load_first = pltpu.make_async_copy(first_hbm, first, local_sem.at[1])
    load_second = pltpu.make_async_copy(
        second_hbm, second.at[pl.ds(0, blocks_here * near2)], local_sem.at[2]
    )
    for i in range(tiles):
        load_plan(i).start()
    load_first.start()
    load_second.start()

    barrier = pltpu.get_barrier_semaphore()
    for oc in range(C):
        for oh in range(PAN):
            if oc or oh:
                pl.semaphore_signal(
                    barrier,
                    inc=1,
                    device_id=(row, ahead(oc), other if oh else pan),
                    device_id_type=MESH,
                )
    for o in range(1, R_AXIS):
        pl.semaphore_signal(
            barrier, inc=1, device_id=(row_ahead(o), me, pan), device_id_type=MESH
        )

    names[me] = jnp.zeros((8, 128), jnp.int32)
    names[me, 0:1, 0:slots] = names_vmem[...]
    second[blocks_here * near2] = jnp.zeros((block, half), jnp.bfloat16)

    def own_name(s):
        return names_smem[0, s]

    for d in range(C):
        for rank in range(CAP):
            slot_of[d * CAP + rank] = ranked_slot(own_name, slots, blocks_here, d, rank)
    for s in range(slots):
        panel = lax.div(own_name(s), jnp.int32(blocks_here))
        rank = jnp.int32(0)
        for t in range(s):
            rank = rank + (lax.div(own_name(t), jnp.int32(blocks_here)) == panel).astype(jnp.int32)
        item_of[0, s] = panel
        item_of[1, s] = jnp.minimum(rank, CAP - 1)
        item_of[2, s] = lax.rem(own_name(s), jnp.int32(blocks_here))

    def relayout(i, carry):
        load_plan(i).wait()
        wide[...] = plan[i].astype(jnp.float32).reshape(block * slots, half)
        for s in range(slots):
            lane = wide[pl.ds(s, block, stride=slots), :]
            tm[i, :, s * half : (s + 1) * half] = lane.astype(jnp.bfloat16)
        return carry

    lax.fori_loop(0, tiles, relayout, 0)

    pl.semaphore_wait(barrier, C * PAN - 1 + R_AXIS - 1)

    def send_names(o):
        return pltpu.make_async_remote_copy(
            src_ref=names.at[me],
            dst_ref=names.at[me],
            send_sem=name_send.at[o],
            recv_sem=name_recv.at[o],
            device_id=(row, ahead(o), pan),
            device_id_type=MESH,
        )

    def take_names(o):
        src = behind(o)
        return pltpu.make_async_remote_copy(
            src_ref=names.at[src],
            dst_ref=names.at[src],
            send_sem=name_send.at[o],
            recv_sem=name_recv.at[o],
            device_id=(row, src, pan),
            device_id_type=MESH,
        )

    for o in range(1, C):
        send_names(o).start()

    def dispatch(i, o):
        return pltpu.make_async_remote_copy(
            src_ref=outgoing.at[i, ahead(o)],
            dst_ref=arrived.at[pan, i, me],
            send_sem=out_send.at[i, o],
            recv_sem=out_recv.at[i, o],
            device_id=(row, ahead(o), pan),
            device_id_type=MESH,
        )

    def arrival(i, o):
        return pltpu.make_async_remote_copy(
            src_ref=outgoing.at[i, behind(o)],
            dst_ref=arrived.at[pan, i, behind(o)],
            send_sem=out_send.at[i, o],
            recv_sem=out_recv.at[i, o],
            device_id=(row, behind(o), pan),
            device_id_type=MESH,
        )

    def share(i, o):
        return pltpu.make_async_remote_copy(
            src_ref=arrived.at[pan, i, behind(o)],
            dst_ref=arrived.at[pan, i, behind(o)],
            send_sem=pan_send.at[i, o],
            recv_sem=pan_recv.at[i, o],
            device_id=(row, me, other),
            device_id_type=MESH,
        )

    def shared(i, o):
        return pltpu.make_async_remote_copy(
            src_ref=arrived.at[other, i, behind(o)],
            dst_ref=arrived.at[other, i, behind(o)],
            send_sem=pan_send.at[i, o],
            recv_sem=pan_recv.at[i, o],
            device_id=(row, me, other),
            device_id_type=MESH,
        )

    def give_back(i, o):
        return pltpu.make_async_remote_copy(
            src_ref=outgoing.at[i, ahead(o)],
            dst_ref=home[i].at[me],
            send_sem=back_send.at[i, o],
            recv_sem=back_recv.at[i, o],
            device_id=(row, ahead(o), pan),
            device_id_type=MESH,
        )

    def got_back(i, o):
        return pltpu.make_async_remote_copy(
            src_ref=outgoing.at[i, behind(o)],
            dst_ref=home[i].at[behind(o)],
            send_sem=back_send.at[i, o],
            recv_sem=back_recv.at[i, o],
            device_id=(row, behind(o), pan),
            device_id_type=MESH,
        )

    load_first.wait()

    def first_step(i, carry):
        left = jnp.concatenate([first[i, q] for q in range(near1)], axis=1)
        step = 2 * half
        for n in range(slots * half // step):
            right = jnp.concatenate(
                [tm[near_smem[i, q], :, n * step : (n + 1) * step] for q in range(near1)], axis=0
            )
            piece = jnp.dot(left, right, preferred_element_type=jnp.float32).astype(jnp.bfloat16)
            product[2 * n] = piece[:, :half]
            product[2 * n + 1] = piece[:, half:]
        for o in list(range(1, C)) + [0]:
            d = ahead(o)
            for rank in range(CAP):
                slot = slot_of[d * CAP + rank]
                piece = product[jnp.maximum(slot, 0)]
                keep = (slot >= 0).astype(jnp.float32).astype(jnp.bfloat16)
                piece = piece if items == slots else piece * keep
                if o:
                    outgoing[i, d, rank] = piece
                else:
                    arrived[pan, i, me, rank] = piece
            if o:
                dispatch(i, o).start()
            else:
                share(i, 0).start()
        return carry

    lax.fori_loop(0, tiles, first_step, 0)

    for o in range(1, C):
        take_names(o).wait_recv()
    copy_names = pltpu.make_async_copy(names, names_all, local_sem.at[3])
    copy_names.start()
    copy_names.wait()
    for src in range(C):
        for rank in range(CAP):
            read = lambda s: names_all[src, 0, s]
            slot = ranked_slot(read, slots, blocks_here, me, rank)
            name = lax.rem(read(jnp.maximum(slot, 0)), jnp.int32(blocks_here))
            label_of[src * CAP + rank] = jnp.where(slot >= 0, name, jnp.int32(-1))
    for l in range(blocks_here):
        hits = jnp.int32(0)
        for t in range(items):
            hits = hits + (label_of[t] == l).astype(jnp.int32)
        present_of[l] = jnp.minimum(hits, 1)

    def index_step(k, carry):
        for l in range(blocks_here):
            found = jnp.int32(blocks_here * near2)
            for q in range(near2):
                found = jnp.where(near_second_smem[k, q] == l, k * near2 + q, found)
            second_index[k, l] = found
        return carry

    lax.fori_loop(0, blocks_here, index_step, 0)
    load_second.wait()

    def spread(line):
        return jnp.transpose(jnp.broadcast_to(line, (half, block)))

    def sums_out(i, oc, oh):
        mine = me * PAN + pan
        return pltpu.make_async_remote_copy(
            src_ref=row_sums.at[mine, i],
            dst_ref=row_sums.at[mine, i],
            send_sem=sum_send.at[i, oc * PAN + oh],
            recv_sem=sum_recv.at[i, oc * PAN + oh],
            device_id=(row, ahead(oc), other if oh else pan),
            device_id_type=MESH,
        )

    def sums_in(i, oc, oh):
        theirs = behind(oc) * PAN + (other if oh else pan)
        return pltpu.make_async_remote_copy(
            src_ref=row_sums.at[theirs, i],
            dst_ref=row_sums.at[theirs, i],
            send_sem=sum_send.at[i, oc * PAN + oh],
            recv_sem=sum_recv.at[i, oc * PAN + oh],
            device_id=(row, behind(oc), other if oh else pan),
            device_id_type=MESH,
        )

    peers = [(oc, oh) for oc in range(C) for oh in range(PAN) if oc or oh]

    def send_home(i):
        for o in range(1, C):
            give_back(i, o).start()

    held = list(range(tiles - 1))

    def release():
        if held:
            send_home(held.pop(0))

    def second_step(i, carry, last=False):
        if last:
            release()
        for o in range(1, C):
            arrival(i, o).wait_recv()
            share(i, o).start()
        if last:
            release()
        for o in range(C):
            shared(i, o).wait_recv()
        at = pl.ds(pl.multiple_of(i * block, block), block)
        first_offset = spread(offset_first[:, at])
        labels = [jnp.maximum(label_of[t], 0) for t in range(items)]
        total = jnp.zeros((block, half), jnp.float32)
        for pair in range(blocks_here // 2):
            crossed = None
            for start in range(0, items, GROUP):
                group = range(start, min(start + GROUP, items))
                left = jnp.concatenate(
                    [arrived[p, i, t // CAP, t % CAP] for t in group for p in range(PAN)], axis=1
                )
                right = jnp.concatenate(
                    [
                        jnp.concatenate(
                            [second[second_index[labels[t], 2 * pair + e]] for e in range(2)],
                            axis=1,
                        )
                        for t in group
                    ],
                    axis=0,
                )
                part = jnp.dot(left, right, preferred_element_type=jnp.float32)
                crossed = part if crossed is None else crossed + part
            for e in range(2):
                l = 2 * pair + e
                here = crossed[:, e * half : (e + 1) * half]
                seen = present_of[l].astype(jnp.float32)
                value = seen * jnp.exp(here - first_offset - offset_second[l : l + 1, :])
                values[l, at, :] = value
                total = total + value
        row_sums[me * PAN + pan, i] = jnp.sum(jnp.transpose(total), axis=0, keepdims=True)
        for oc, oh in peers:
            sums_out(i, oc, oh).start()
        for o in range(1, C):
            dispatch(i, o).wait_send()
        for d in range(C):
            for rank in range(CAP):
                label = jnp.maximum(label_of[d * CAP + rank], 0)
                value = jnp.minimum(values[label, at, :], BF16_MAX).astype(jnp.bfloat16)
                outgoing[i, d, rank] = value
        return carry

    lax.fori_loop(0, tiles - 1, second_step, 0)
    second_step(tiles - 1, 0, last=True)
    held.append(tiles - 1)
    release()
    for i in range(tiles):
        for oc, oh in peers:
            sums_in(i, oc, oh).wait_recv()
    width = float(slots * C * block)
    for i in range(tiles):
        part = slice(i * block, (i + 1) * block)
        totals = row_sums[0, i]
        for t in range(1, C * PAN):
            totals = totals + row_sums[t, i]
        scale_first_ref[:, part] = weight_first[:, part] * width / totals

    def col_step(i, sums):
        at = pl.ds(pl.multiple_of(i * block, block), block)
        scale = spread(scale_first_ref[:, at])
        row_scale[at, :] = scale
        return tuple(
            sums[l] + jnp.sum(values[l, at, :] * scale, axis=0, keepdims=True)
            for l in range(blocks_here)
        )

    sums = lax.fori_loop(
        0, tiles, col_step, tuple(jnp.zeros((1, half), jnp.float32) for _ in range(blocks_here))
    )
    for l in range(blocks_here):
        col_sums[row, l : l + 1, :] = sums[l]
        col_sums[row, blocks_here + l : blocks_here + l + 1, :] = jnp.full(
            (1, half), present_of[l].astype(jnp.float32) * float(rows_total), jnp.float32
        )

    def cols_out(o):
        return pltpu.make_async_remote_copy(
            src_ref=col_sums.at[row],
            dst_ref=col_sums.at[row],
            send_sem=col_send.at[o],
            recv_sem=col_recv.at[o],
            device_id=(row_ahead(o), me, pan),
            device_id_type=MESH,
        )

    def cols_in(o):
        return pltpu.make_async_remote_copy(
            src_ref=col_sums.at[row_behind(o)],
            dst_ref=col_sums.at[row_behind(o)],
            send_sem=col_send.at[o],
            recv_sem=col_recv.at[o],
            device_id=(row_behind(o), me, pan),
            device_id_type=MESH,
        )

    for o in range(1, R_AXIS):
        cols_out(o).start()
    release()
    for i in range(tiles):
        home[i][me] = outgoing[i, me]
    for o in range(1, R_AXIS):
        cols_in(o).wait_recv()
    both = col_sums[0]
    for t in range(1, R_AXIS):
        both = both + col_sums[t]
    colsum, counts = both[:blocks_here], both[blocks_here:]
    scale_second = weight_second[...] * counts / jnp.where(counts > 0, colsum, 1.0)
    scale_second_ref[...] = scale_second
    scales[me] = scale_second

    def scale_out(o):
        return pltpu.make_async_remote_copy(
            src_ref=scales.at[me],
            dst_ref=scales.at[me],
            send_sem=scale_send.at[o],
            recv_sem=scale_recv.at[o],
            device_id=(row, ahead(o), pan),
            device_id_type=MESH,
        )

    def scale_in(o):
        return pltpu.make_async_remote_copy(
            src_ref=scales.at[behind(o)],
            dst_ref=scales.at[behind(o)],
            send_sem=scale_send.at[o],
            recv_sem=scale_recv.at[o],
            device_id=(row, behind(o), pan),
            device_id_type=MESH,
        )

    for o in range(1, C):
        scale_out(o).start()
    while held:
        release()
    for o in range(1, C):
        scale_in(o).wait_recv()

    def store(i):
        return pltpu.make_async_copy(
            finished.at[i], out_ref.at[pl.ds(i * block, block)], done_sem.at[i]
        )

    for i in range(tiles):
        for o in range(1, C):
            got_back(i, o).wait_recv()
        scale = row_scale[i * block : (i + 1) * block, :]
        for s in range(slots):
            panel, rank, name = item_of[0, s], item_of[1, s], item_of[2, s]
            value = home[i][panel, rank].astype(jnp.float32) * scale
            value = value * scales[panel, pl.ds(name, 1), :]
            wide[pl.ds(s, block, stride=slots), :] = value
        finished[i] = wide[...].reshape(block, slots, half).astype(jnp.bfloat16)
        store(i).start()

    def drain(i, carry):
        for o in range(C):
            share(i, o).wait_send()
        for oc, oh in peers:
            sums_out(i, oc, oh).wait_send()
        return carry

    lax.fori_loop(0, tiles, drain, 0)
    for i in range(tiles):
        for o in range(1, C):
            give_back(i, o).wait_send()
    for o in range(1, C):
        send_names(o).wait_send()
        scale_out(o).wait_send()
    for o in range(1, R_AXIS):
        cols_out(o).wait_send()
    for i in range(tiles):
        store(i).wait()


def hand_out(plan_in, first_in, second_in, plan_out, first_out, second_out, sems):
    pieces = sems.shape[0] - 2
    rows = plan_in.shape[0] // pieces
    copies = [
        pltpu.make_async_copy(
            plan_in.at[pl.ds(i * rows, rows)], plan_out.at[pl.ds(i * rows, rows)], sems.at[i]
        )
        for i in range(pieces)
    ]
    copies.append(pltpu.make_async_copy(first_in, first_out, sems.at[pieces]))
    copies.append(pltpu.make_async_copy(second_in, second_out, sems.at[pieces + 1]))
    for copy in copies:
        copy.start()
    for copy in copies:
        copy.wait()


def local(
    plan_values,
    plan_blocks,
    first_values,
    first_blocks,
    second_values,
    second_blocks,
    weight_first,
    weight_second,
    offset_first,
    offset_second,
):
    C, R_AXIS = lax.axis_size("col"), lax.axis_size("row")
    rows, slots, half = plan_values.shape
    tiles, near1, block, _ = first_values.shape
    blocks_here, near2 = second_blocks.shape
    dims = (C, R_AXIS, tiles, block, slots, half, blocks_here, near1, near2)
    bf16, f32, i32 = jnp.bfloat16, jnp.float32, jnp.int32
    vmem, smem = pltpu.VMEM, pltpu.SMEM
    dma = pltpu.SemaphoreType.DMA
    in_vmem, in_smem = pl.BlockSpec(memory_space=vmem), pl.BlockSpec(memory_space=smem)
    anywhere = pl.BlockSpec(memory_space=pl.ANY)
    out, scale_first, scale_second = pl.pallas_call(
        functools.partial(kernel, dims),
        out_shape=(
            jax.ShapeDtypeStruct((rows, slots, half), bf16),
            jax.ShapeDtypeStruct((1, rows), f32),
            jax.ShapeDtypeStruct((blocks_here, half), f32),
        ),
        in_specs=[
            anywhere,
            in_smem,
            in_vmem,
            anywhere,
            in_smem,
            anywhere,
            in_smem,
            in_vmem,
            in_vmem,
            in_vmem,
            in_vmem,
        ],
        out_specs=(anywhere, in_vmem, in_vmem),
        scratch_shapes=[
            vmem((tiles, block, slots, half), bf16),
            vmem((block * slots, half), f32),
            vmem((tiles, block, slots * half), bf16),
            vmem((tiles, near1, block, block), bf16),
            vmem((blocks_here * near2 + 1, block, half), bf16),
            vmem((slots, block, half), bf16),
            vmem((tiles, C, CAP, block, half), bf16),
            vmem((PAN, tiles, C, CAP, block, half), bf16),
            vmem((blocks_here, rows, half), f32),
            vmem((tiles, block, slots, half), bf16),
            vmem((C * PAN, tiles, 1, block), f32),
            vmem((R_AXIS, 2 * blocks_here, half), f32),
            vmem((C, blocks_here, half), f32),
            vmem((C, 8, 128), i32),
            vmem((rows, half), f32),
            smem((C, 8, 128), i32),
            smem((blocks_here, blocks_here), i32),
            smem((C * CAP,), i32),
            smem((C * CAP,), i32),
            smem((blocks_here,), i32),
            smem((3, slots), i32),
            dma((4,)),
            dma((C,)),
            dma((C,)),
            dma((tiles, C)),
            dma((tiles, C)),
            dma((tiles, C)),
            dma((tiles, C)),
            dma((tiles, C)),
            dma((tiles, C)),
            dma((tiles, C * PAN)),
            dma((tiles, C * PAN)),
            dma((R_AXIS,)),
            dma((R_AXIS,)),
            dma((C,)),
            dma((C,)),
            dma((tiles,)),
            dma((tiles,)),
        ]
        + [vmem((C, CAP, block, half), bf16)] * tiles,
        compiler_params=pltpu.CompilerParams(
            collective_id=0, has_side_effects=True, vmem_limit_bytes=60 * 1024 * 1024
        ),
        name="gromov_step",
    )(
        plan_values,
        plan_blocks,
        plan_blocks,
        first_values,
        first_blocks,
        second_values.reshape(blocks_here * near2, block, half),
        second_blocks,
        weight_first.reshape(1, rows),
        weight_second,
        offset_first.reshape(1, rows),
        offset_second,
    )
    results = (out, scale_first, scale_second)
    out, scale_first, scale_second = pl.pallas_call(
        hand_out,
        out_shape=tuple(jax.ShapeDtypeStruct(r.shape, r.dtype) for r in results),
        in_specs=[anywhere] * 3,
        out_specs=(anywhere,) * 3,
        scratch_shapes=[dma((2 * tiles + 2,))],
        name="hand_out",
    )(*results)
    return out, scale_first.reshape(rows), scale_second


def solution(mesh):
    return jax.shard_map(
        local,
        mesh=mesh,
        in_specs=(
            P("row", "col", "pan"),
            P("row", "col"),
            P("row", None, None, None),
            P("row", None),
            P("col", None, None, "pan"),
            P("col", None),
            P("row"),
            P("col", "pan"),
            P("row"),
            P("col", "pan"),
        ),
        out_specs=(P("row", "col", "pan"), P("row"), P("col", "pan")),
        check_vma=False,
    )
```

```python
import functools

import jax
import jax.numpy as jnp
from jax import lax
from jax.experimental import pallas as pl
from jax.experimental.pallas import tpu as pltpu
from jax.sharding import PartitionSpec as P

CAP = 2
PAN = 2
GROUP = 8
MESH = pl.DeviceIdType.MESH
BF16_MAX = float(jnp.finfo(jnp.bfloat16).max)


def ranked_slot(read, slots, blocks_here, panel, rank):
    seen, found = jnp.int32(0), jnp.int32(-1)
    for s in range(slots):
        match = (lax.div(read(s), jnp.int32(blocks_here)) == panel).astype(jnp.int32)
        hit = match * (seen == rank).astype(jnp.int32)
        found = jnp.where(hit > 0, jnp.int32(s), found)
        seen = seen + match
    return found


def kernel(
    dims,
    plan_hbm,
    names_smem,
    names_vmem,
    first_hbm,
    near_smem,
    second_hbm,
    near_second_smem,
    weight_first,
    weight_second,
    offset_first,
    offset_second,
    out_ref,
    scale_first_ref,
    scale_second_ref,
    plan,
    wide,
    tm,
    first,
    second,
    product,
    outgoing,
    arrived,
    values,
    finished,
    row_sums,
    col_sums,
    scales,
    names,
    row_scale,
    names_all,
    second_index,
    slot_of,
    label_of,
    present_of,
    item_of,
    local_sem,
    name_send,
    name_recv,
    out_send,
    out_recv,
    pan_send,
    pan_recv,
    back_send,
    back_recv,
    sum_send,
    sum_recv,
    col_send,
    col_recv,
    scale_send,
    scale_recv,
    plan_sem,
    done_sem,
    *home,
):
    C, R_AXIS, tiles, block, slots, half, blocks_here, near1, near2 = dims
    rows_total = tiles * block
    items = C * CAP
    row, me, pan = lax.axis_index("row"), lax.axis_index("col"), lax.axis_index("pan")
    other = 1 - pan

    def ahead(o):
        return lax.rem(me + o, C)

    def behind(o):
        return lax.rem(me - o + C, C)

    def row_ahead(o):
        return lax.rem(row + o, R_AXIS)

    def row_behind(o):
        return lax.rem(row - o + R_AXIS, R_AXIS)

    def load_plan(i):
        return pltpu.make_async_copy(
            plan_hbm.at[pl.ds(i * block, block)], plan.at[i], plan_sem.at[i]
        )

    load_first = pltpu.make_async_copy(first_hbm, first, local_sem.at[1])
    load_second = pltpu.make_async_copy(
        second_hbm, second.at[pl.ds(0, blocks_here * near2)], local_sem.at[2]
    )
    for i in range(tiles):
        load_plan(i).start()
    load_first.start()
    load_second.start()

    barrier = pltpu.get_barrier_semaphore()
    for oc in range(C):
        for oh in range(PAN):
            if oc or oh:
                pl.semaphore_signal(
                    barrier,
                    inc=1,
                    device_id=(row, ahead(oc), other if oh else pan),
                    device_id_type=MESH,
                )
    for o in range(1, R_AXIS):
        pl.semaphore_signal(
            barrier, inc=1, device_id=(row_ahead(o), me, pan), device_id_type=MESH
        )

    names[me] = jnp.zeros((8, 128), jnp.int32)
    names[me, 0:1, 0:slots] = names_vmem[...]
    second[blocks_here * near2] = jnp.zeros((block, half), jnp.bfloat16)

    def own_name(s):
        return names_smem[0, s]

    for d in range(C):
        for rank in range(CAP):
            slot_of[d * CAP + rank] = ranked_slot(own_name, slots, blocks_here, d, rank)
    for s in range(slots):
        panel = lax.div(own_name(s), jnp.int32(blocks_here))
        rank = jnp.int32(0)
        for t in range(s):
            rank = rank + (lax.div(own_name(t), jnp.int32(blocks_here)) == panel).astype(jnp.int32)
        item_of[0, s] = panel
        item_of[1, s] = jnp.minimum(rank, CAP - 1)
        item_of[2, s] = lax.rem(own_name(s), jnp.int32(blocks_here))

    def relayout(i, carry):
        load_plan(i).wait()
        wide[...] = plan[i].astype(jnp.float32).reshape(block * slots, half)
        for s in range(slots):
            lane = wide[pl.ds(s, block, stride=slots), :]
            tm[i, :, s * half : (s + 1) * half] = lane.astype(jnp.bfloat16)
        return carry

    lax.fori_loop(0, tiles, relayout, 0)

    pl.semaphore_wait(barrier, C * PAN - 1 + R_AXIS - 1)

    def send_names(o):
        return pltpu.make_async_remote_copy(
            src_ref=names.at[me],
            dst_ref=names.at[me],
            send_sem=name_send.at[o],
            recv_sem=name_recv.at[o],
            device_id=(row, ahead(o), pan),
            device_id_type=MESH,
        )

    def take_names(o):
        src = behind(o)
        return pltpu.make_async_remote_copy(
            src_ref=names.at[src],
            dst_ref=names.at[src],
            send_sem=name_send.at[o],
            recv_sem=name_recv.at[o],
            device_id=(row, src, pan),
            device_id_type=MESH,
        )

    for o in range(1, C):
        send_names(o).start()

    def dispatch(i, o):
        return pltpu.make_async_remote_copy(
            src_ref=outgoing.at[i, ahead(o)],
            dst_ref=arrived.at[pan, i, me],
            send_sem=out_send.at[i, o],
            recv_sem=out_recv.at[i, o],
            device_id=(row, ahead(o), pan),
            device_id_type=MESH,
        )

    def arrival(i, o):
        return pltpu.make_async_remote_copy(
            src_ref=outgoing.at[i, behind(o)],
            dst_ref=arrived.at[pan, i, behind(o)],
            send_sem=out_send.at[i, o],
            recv_sem=out_recv.at[i, o],
            device_id=(row, behind(o), pan),
            device_id_type=MESH,
        )

    def share(i, o):
        return pltpu.make_async_remote_copy(
            src_ref=arrived.at[pan, i, behind(o)],
            dst_ref=arrived.at[pan, i, behind(o)],
            send_sem=pan_send.at[i, o],
            recv_sem=pan_recv.at[i, o],
            device_id=(row, me, other),
            device_id_type=MESH,
        )

    def shared(i, o):
        return pltpu.make_async_remote_copy(
            src_ref=arrived.at[other, i, behind(o)],
            dst_ref=arrived.at[other, i, behind(o)],
            send_sem=pan_send.at[i, o],
            recv_sem=pan_recv.at[i, o],
            device_id=(row, me, other),
            device_id_type=MESH,
        )

    def give_back(i, o):
        return pltpu.make_async_remote_copy(
            src_ref=outgoing.at[i, ahead(o)],
            dst_ref=home[i].at[me],
            send_sem=back_send.at[i, o],
            recv_sem=back_recv.at[i, o],
            device_id=(row, ahead(o), pan),
            device_id_type=MESH,
        )

    def got_back(i, o):
        return pltpu.make_async_remote_copy(
            src_ref=outgoing.at[i, behind(o)],
            dst_ref=home[i].at[behind(o)],
            send_sem=back_send.at[i, o],
            recv_sem=back_recv.at[i, o],
            device_id=(row, behind(o), pan),
            device_id_type=MESH,
        )

    load_first.wait()

    def first_step(i, carry):
        left = jnp.concatenate([first[i, q] for q in range(near1)], axis=1)
        step = 2 * half
        for n in range(slots * half // step):
            right = jnp.concatenate(
                [tm[near_smem[i, q], :, n * step : (n + 1) * step] for q in range(near1)], axis=0
            )
            piece = jnp.dot(left, right, preferred_element_type=jnp.float32).astype(jnp.bfloat16)
            product[2 * n] = piece[:, :half]
            product[2 * n + 1] = piece[:, half:]
        for o in list(range(1, C)) + [0]:
            d = ahead(o)
            for rank in range(CAP):
                slot = slot_of[d * CAP + rank]
                piece = product[jnp.maximum(slot, 0)]
                keep = (slot >= 0).astype(jnp.float32).astype(jnp.bfloat16)
                piece = piece if items == slots else piece * keep
                if o:
                    outgoing[i, d, rank] = piece
                else:
                    arrived[pan, i, me, rank] = piece
            if o:
                dispatch(i, o).start()
            else:
                share(i, 0).start()
        return carry

    lax.fori_loop(0, tiles, first_step, 0)

    for o in range(1, C):
        take_names(o).wait_recv()
    copy_names = pltpu.make_async_copy(names, names_all, local_sem.at[3])
    copy_names.start()
    copy_names.wait()
    for src in range(C):
        for rank in range(CAP):
            read = lambda s: names_all[src, 0, s]
            slot = ranked_slot(read, slots, blocks_here, me, rank)
            name = lax.rem(read(jnp.maximum(slot, 0)), jnp.int32(blocks_here))
            label_of[src * CAP + rank] = jnp.where(slot >= 0, name, jnp.int32(-1))
    for l in range(blocks_here):
        hits = jnp.int32(0)
        for t in range(items):
            hits = hits + (label_of[t] == l).astype(jnp.int32)
        present_of[l] = jnp.minimum(hits, 1)

    def index_step(k, carry):
        for l in range(blocks_here):
            found = jnp.int32(blocks_here * near2)
            for q in range(near2):
                found = jnp.where(near_second_smem[k, q] == l, k * near2 + q, found)
            second_index[k, l] = found
        return carry

    lax.fori_loop(0, blocks_here, index_step, 0)
    load_second.wait()

    def spread(line):
        return jnp.transpose(jnp.broadcast_to(line, (half, block)))

    def sums_out(i, oc, oh):
        mine = me * PAN + pan
        return pltpu.make_async_remote_copy(
            src_ref=row_sums.at[mine, i],
            dst_ref=row_sums.at[mine, i],
            send_sem=sum_send.at[i, oc * PAN + oh],
            recv_sem=sum_recv.at[i, oc * PAN + oh],
            device_id=(row, ahead(oc), other if oh else pan),
            device_id_type=MESH,
        )

    def sums_in(i, oc, oh):
        theirs = behind(oc) * PAN + (other if oh else pan)
        return pltpu.make_async_remote_copy(
            src_ref=row_sums.at[theirs, i],
            dst_ref=row_sums.at[theirs, i],
            send_sem=sum_send.at[i, oc * PAN + oh],
            recv_sem=sum_recv.at[i, oc * PAN + oh],
            device_id=(row, behind(oc), other if oh else pan),
            device_id_type=MESH,
        )

    peers = [(oc, oh) for oc in range(C) for oh in range(PAN) if oc or oh]

    def send_home(i):
        for o in range(1, C):
            give_back(i, o).start()

    def forward(i):
        for o in range(1, C):
            arrival(i, o).wait_recv()
            share(i, o).start()

    held = list(range(tiles))

    def release():
        if held:
            send_home(held.pop(0))

    def stage(i):
        at = pl.ds(pl.multiple_of(i * block, block), block)
        for o in range(1, C):
            dispatch(i, o).wait_send()
        for d in range(C):
            for rank in range(CAP):
                label = jnp.maximum(label_of[d * CAP + rank], 0)
                value = jnp.minimum(values[label, at, :], BF16_MAX).astype(jnp.bfloat16)
                outgoing[i, d, rank] = value

    def second_step(i, carry):
        for o in range(C):
            shared(i, o).wait_recv()
        at = pl.ds(pl.multiple_of(i * block, block), block)
        first_offset = spread(offset_first[:, at])
        labels = [jnp.maximum(label_of[t], 0) for t in range(items)]
        total = jnp.zeros((block, half), jnp.float32)
        for pair in range(blocks_here // 2):
            crossed = None
            for start in range(0, items, GROUP):
                group = range(start, min(start + GROUP, items))
                left = jnp.concatenate(
                    [arrived[p, i, t // CAP, t % CAP] for t in group for p in range(PAN)], axis=1
                )
                right = jnp.concatenate(
                    [
                        jnp.concatenate(
                            [second[second_index[labels[t], 2 * pair + e]] for e in range(2)],
                            axis=1,
                        )
                        for t in group
                    ],
                    axis=0,
                )
                part = jnp.dot(left, right, preferred_element_type=jnp.float32)
                crossed = part if crossed is None else crossed + part
            for e in range(2):
                l = 2 * pair + e
                here = crossed[:, e * half : (e + 1) * half]
                seen = present_of[l].astype(jnp.float32)
                value = seen * jnp.exp(here - first_offset - offset_second[l : l + 1, :])
                values[l, at, :] = value
                total = total + value
        row_sums[me * PAN + pan, i] = jnp.sum(jnp.transpose(total), axis=0, keepdims=True)
        for oc, oh in peers:
            sums_out(i, oc, oh).start()
        return carry

    def middle_step(i, carry):
        second_step(i, 0)
        forward(i + 1)
        stage(i)
        return carry

    forward(0)
    lax.fori_loop(0, tiles - 2, middle_step, 0)
    second_step(tiles - 2, 0)
    release()
    forward(tiles - 1)
    stage(tiles - 2)
    release()
    second_step(tiles - 1, 0)
    release()
    stage(tiles - 1)
    for i in range(tiles):
        for oc, oh in peers:
            sums_in(i, oc, oh).wait_recv()
    width = float(slots * C * block)
    for i in range(tiles):
        part = slice(i * block, (i + 1) * block)
        totals = row_sums[0, i]
        for t in range(1, C * PAN):
            totals = totals + row_sums[t, i]
        scale_first_ref[:, part] = weight_first[:, part] * width / totals

    def col_step(i, sums):
        at = pl.ds(pl.multiple_of(i * block, block), block)
        scale = spread(scale_first_ref[:, at])
        row_scale[at, :] = scale
        return tuple(
            sums[l] + jnp.sum(values[l, at, :] * scale, axis=0, keepdims=True)
            for l in range(blocks_here)
        )

    sums = lax.fori_loop(
        0, tiles, col_step, tuple(jnp.zeros((1, half), jnp.float32) for _ in range(blocks_here))
    )
    for l in range(blocks_here):
        col_sums[row, l : l + 1, :] = sums[l]
        col_sums[row, blocks_here + l : blocks_here + l + 1, :] = jnp.full(
            (1, half), present_of[l].astype(jnp.float32) * float(rows_total), jnp.float32
        )

    def cols_out(o):
        return pltpu.make_async_remote_copy(
            src_ref=col_sums.at[row],
            dst_ref=col_sums.at[row],
            send_sem=col_send.at[o],
            recv_sem=col_recv.at[o],
            device_id=(row_ahead(o), me, pan),
            device_id_type=MESH,
        )

    def cols_in(o):
        return pltpu.make_async_remote_copy(
            src_ref=col_sums.at[row_behind(o)],
            dst_ref=col_sums.at[row_behind(o)],
            send_sem=col_send.at[o],
            recv_sem=col_recv.at[o],
            device_id=(row_behind(o), me, pan),
            device_id_type=MESH,
        )

    for o in range(1, R_AXIS):
        cols_out(o).start()
    release()
    for i in range(tiles):
        home[i][me] = outgoing[i, me]
    for o in range(1, R_AXIS):
        cols_in(o).wait_recv()
    both = col_sums[0]
    for t in range(1, R_AXIS):
        both = both + col_sums[t]
    colsum, counts = both[:blocks_here], both[blocks_here:]
    scale_second = weight_second[...] * counts / jnp.where(counts > 0, colsum, 1.0)
    scale_second_ref[...] = scale_second
    scales[me] = scale_second

    def scale_out(o):
        return pltpu.make_async_remote_copy(
            src_ref=scales.at[me],
            dst_ref=scales.at[me],
            send_sem=scale_send.at[o],
            recv_sem=scale_recv.at[o],
            device_id=(row, ahead(o), pan),
            device_id_type=MESH,
        )

    def scale_in(o):
        return pltpu.make_async_remote_copy(
            src_ref=scales.at[behind(o)],
            dst_ref=scales.at[behind(o)],
            send_sem=scale_send.at[o],
            recv_sem=scale_recv.at[o],
            device_id=(row, behind(o), pan),
            device_id_type=MESH,
        )

    for o in range(1, C):
        scale_out(o).start()
    while held:
        release()
    for o in range(1, C):
        scale_in(o).wait_recv()

    def store(i):
        return pltpu.make_async_copy(
            finished.at[i], out_ref.at[pl.ds(i * block, block)], done_sem.at[i]
        )

    for i in range(tiles):
        for o in range(1, C):
            got_back(i, o).wait_recv()
        scale = row_scale[i * block : (i + 1) * block, :]
        for s in range(slots):
            panel, rank, name = item_of[0, s], item_of[1, s], item_of[2, s]
            value = home[i][panel, rank].astype(jnp.float32) * scale
            value = value * scales[panel, pl.ds(name, 1), :]
            wide[pl.ds(s, block, stride=slots), :] = value
        finished[i] = wide[...].reshape(block, slots, half).astype(jnp.bfloat16)
        store(i).start()

    def drain(i, carry):
        for o in range(C):
            share(i, o).wait_send()
        for oc, oh in peers:
            sums_out(i, oc, oh).wait_send()
        return carry

    lax.fori_loop(0, tiles, drain, 0)
    for i in range(tiles):
        for o in range(1, C):
            give_back(i, o).wait_send()
    for o in range(1, C):
        send_names(o).wait_send()
        scale_out(o).wait_send()
    for o in range(1, R_AXIS):
        cols_out(o).wait_send()
    for i in range(tiles):
        store(i).wait()


def hand_out(plan_in, first_in, second_in, plan_out, first_out, second_out):
    plan_out[...] = plan_in[...]
    first_out[...] = first_in[...]
    second_out[...] = second_in[...]


def local(
    plan_values,
    plan_blocks,
    first_values,
    first_blocks,
    second_values,
    second_blocks,
    weight_first,
    weight_second,
    offset_first,
    offset_second,
):
    C, R_AXIS = lax.axis_size("col"), lax.axis_size("row")
    rows, slots, half = plan_values.shape
    tiles, near1, block, _ = first_values.shape
    blocks_here, near2 = second_blocks.shape
    dims = (C, R_AXIS, tiles, block, slots, half, blocks_here, near1, near2)
    bf16, f32, i32 = jnp.bfloat16, jnp.float32, jnp.int32
    vmem, smem = pltpu.VMEM, pltpu.SMEM
    dma = pltpu.SemaphoreType.DMA
    in_vmem, in_smem = pl.BlockSpec(memory_space=vmem), pl.BlockSpec(memory_space=smem)
    anywhere = pl.BlockSpec(memory_space=pl.ANY)
    out, scale_first, scale_second = pl.pallas_call(
        functools.partial(kernel, dims),
        out_shape=(
            jax.ShapeDtypeStruct((rows, slots, half), bf16),
            jax.ShapeDtypeStruct((1, rows), f32),
            jax.ShapeDtypeStruct((blocks_here, half), f32),
        ),
        in_specs=[
            anywhere,
            in_smem,
            in_vmem,
            anywhere,
            in_smem,
            anywhere,
            in_smem,
            in_vmem,
            in_vmem,
            in_vmem,
            in_vmem,
        ],
        out_specs=(anywhere, in_vmem, in_vmem),
        scratch_shapes=[
            vmem((tiles, block, slots, half), bf16),
            vmem((block * slots, half), f32),
            vmem((tiles, block, slots * half), bf16),
            vmem((tiles, near1, block, block), bf16),
            vmem((blocks_here * near2 + 1, block, half), bf16),
            vmem((slots, block, half), bf16),
            vmem((tiles, C, CAP, block, half), bf16),
            vmem((PAN, tiles, C, CAP, block, half), bf16),
            vmem((blocks_here, rows, half), f32),
            vmem((tiles, block, slots, half), bf16),
            vmem((C * PAN, tiles, 1, block), f32),
            vmem((R_AXIS, 2 * blocks_here, half), f32),
            vmem((C, blocks_here, half), f32),
            vmem((C, 8, 128), i32),
            vmem((rows, half), f32),
            smem((C, 8, 128), i32),
            smem((blocks_here, blocks_here), i32),
            smem((C * CAP,), i32),
            smem((C * CAP,), i32),
            smem((blocks_here,), i32),
            smem((3, slots), i32),
            dma((4,)),
            dma((C,)),
            dma((C,)),
            dma((tiles, C)),
            dma((tiles, C)),
            dma((tiles, C)),
            dma((tiles, C)),
            dma((tiles, C)),
            dma((tiles, C)),
            dma((tiles, C * PAN)),
            dma((tiles, C * PAN)),
            dma((R_AXIS,)),
            dma((R_AXIS,)),
            dma((C,)),
            dma((C,)),
            dma((tiles,)),
            dma((tiles,)),
        ]
        + [vmem((C, CAP, block, half), bf16)] * tiles,
        compiler_params=pltpu.CompilerParams(
            collective_id=0, has_side_effects=True, vmem_limit_bytes=60 * 1024 * 1024
        ),
        name="gromov_step",
    )(
        plan_values,
        plan_blocks,
        plan_blocks,
        first_values,
        first_blocks,
        second_values.reshape(blocks_here * near2, block, half),
        second_blocks,
        weight_first.reshape(1, rows),
        weight_second,
        offset_first.reshape(1, rows),
        offset_second,
    )
    by_tile = pl.BlockSpec((block, slots, half), lambda i: (i, 0, 0))
    whole_first = pl.BlockSpec((1, rows), lambda i: (0, 0))
    whole_second = pl.BlockSpec((blocks_here, half), lambda i: (0, 0))
    results = (out, scale_first, scale_second)
    out, scale_first, scale_second = pl.pallas_call(
        hand_out,
        out_shape=tuple(jax.ShapeDtypeStruct(r.shape, r.dtype) for r in results),
        grid=(tiles,),
        in_specs=[by_tile, whole_first, whole_second],
        out_specs=(by_tile, whole_first, whole_second),
        name="hand_out",
    )(*results)
    return out, scale_first.reshape(rows), scale_second


def solution(mesh):
    return jax.shard_map(
        local,
        mesh=mesh,
        in_specs=(
            P("row", "col", "pan"),
            P("row", "col"),
            P("row", None, None, None),
            P("row", None),
            P("col", None, None, "pan"),
            P("col", None),
            P("row"),
            P("col", "pan"),
            P("row"),
            P("col", "pan"),
        ),
        out_specs=(P("row", "col", "pan"), P("row"), P("col", "pan")),
        check_vma=False,
    )
```

```python
import functools

import jax
import jax.numpy as jnp
from jax import lax
from jax.experimental import pallas as pl
from jax.experimental.pallas import tpu as pltpu
from jax.sharding import PartitionSpec as P

CAP = 2
PAN = 2
GROUP = 8
MESH = pl.DeviceIdType.MESH
BF16_MAX = float(jnp.finfo(jnp.bfloat16).max)


def ranked_slot(read, slots, blocks_here, panel, rank):
    seen, found = jnp.int32(0), jnp.int32(-1)
    for s in range(slots):
        match = (lax.div(read(s), jnp.int32(blocks_here)) == panel).astype(jnp.int32)
        hit = match * (seen == rank).astype(jnp.int32)
        found = jnp.where(hit > 0, jnp.int32(s), found)
        seen = seen + match
    return found


def kernel(
    dims,
    plan_hbm,
    names_smem,
    names_vmem,
    first_hbm,
    near_smem,
    second_hbm,
    near_second_smem,
    weight_first,
    weight_second,
    offset_first,
    offset_second,
    home,
    scale_first_ref,
    scale_second_ref,
    scales_ref,
    plan,
    wide,
    tm,
    first,
    second,
    product,
    outgoing,
    arrived,
    values,
    row_sums,
    col_sums,
    scales,
    names,
    names_all,
    second_index,
    slot_of,
    label_of,
    present_of,
    local_sem,
    name_send,
    name_recv,
    out_send,
    out_recv,
    pan_send,
    pan_recv,
    back_send,
    back_recv,
    sum_send,
    sum_recv,
    col_send,
    col_recv,
    scale_send,
    scale_recv,
    plan_sem,
    first_sem,
    done_sem,
):
    C, R_AXIS, tiles, block, slots, half, blocks_here, near1, near2 = dims
    rows_total = tiles * block
    items = C * CAP
    row, me, pan = lax.axis_index("row"), lax.axis_index("col"), lax.axis_index("pan")
    other = 1 - pan

    def ahead(o):
        return lax.rem(me + o, C)

    def behind(o):
        return lax.rem(me - o + C, C)

    def row_ahead(o):
        return lax.rem(row + o, R_AXIS)

    def row_behind(o):
        return lax.rem(row - o + R_AXIS, R_AXIS)

    def load_plan(i):
        return pltpu.make_async_copy(
            plan_hbm.at[pl.ds(i * block, block)], plan.at[i], plan_sem.at[i]
        )

    def load_first(i):
        return pltpu.make_async_copy(first_hbm.at[i], first.at[i], first_sem.at[i])

    load_second = pltpu.make_async_copy(
        second_hbm, second.at[pl.ds(0, blocks_here * near2)], local_sem.at[2]
    )
    for i in range(tiles):
        load_plan(i).start()
    for i in range(tiles):
        load_first(i).start()

    barrier = pltpu.get_barrier_semaphore()
    for oc in range(C):
        for oh in range(PAN):
            if oc or oh:
                pl.semaphore_signal(
                    barrier,
                    inc=1,
                    device_id=(row, ahead(oc), other if oh else pan),
                    device_id_type=MESH,
                )
    for o in range(1, R_AXIS):
        pl.semaphore_signal(
            barrier, inc=1, device_id=(row_ahead(o), me, pan), device_id_type=MESH
        )

    names[me] = jnp.zeros((8, 128), jnp.int32)
    names[me, 0:1, 0:slots] = names_vmem[...]
    second[blocks_here * near2] = jnp.zeros((block, half), jnp.bfloat16)

    def own_name(s):
        return names_smem[0, s]

    for d in range(C):
        for rank in range(CAP):
            slot_of[d * CAP + rank] = ranked_slot(own_name, slots, blocks_here, d, rank)
    def relayout(i, carry):
        load_plan(i).wait()
        wide[...] = plan[i].astype(jnp.float32).reshape(block * slots, half)
        for s in range(slots):
            lane = wide[pl.ds(s, block, stride=slots), :]
            tm[i, :, s * half : (s + 1) * half] = lane.astype(jnp.bfloat16)
        return carry

    lax.fori_loop(0, tiles, relayout, 0)
    load_second.start()

    pl.semaphore_wait(barrier, C * PAN - 1 + R_AXIS - 1)

    def send_names(o):
        return pltpu.make_async_remote_copy(
            src_ref=names.at[me],
            dst_ref=names.at[me],
            send_sem=name_send.at[o],
            recv_sem=name_recv.at[o],
            device_id=(row, ahead(o), pan),
            device_id_type=MESH,
        )

    def take_names(o):
        src = behind(o)
        return pltpu.make_async_remote_copy(
            src_ref=names.at[src],
            dst_ref=names.at[src],
            send_sem=name_send.at[o],
            recv_sem=name_recv.at[o],
            device_id=(row, src, pan),
            device_id_type=MESH,
        )

    for o in range(1, C):
        send_names(o).start()

    def dispatch(i, o):
        return pltpu.make_async_remote_copy(
            src_ref=outgoing.at[i, ahead(o)],
            dst_ref=arrived.at[pan, i, me],
            send_sem=out_send.at[i, o],
            recv_sem=out_recv.at[i, o],
            device_id=(row, ahead(o), pan),
            device_id_type=MESH,
        )

    def arrival(i, o):
        return pltpu.make_async_remote_copy(
            src_ref=outgoing.at[i, behind(o)],
            dst_ref=arrived.at[pan, i, behind(o)],
            send_sem=out_send.at[i, o],
            recv_sem=out_recv.at[i, o],
            device_id=(row, behind(o), pan),
            device_id_type=MESH,
        )

    def share(i, o):
        return pltpu.make_async_remote_copy(
            src_ref=arrived.at[pan, i, behind(o)],
            dst_ref=arrived.at[pan, i, behind(o)],
            send_sem=pan_send.at[i, o],
            recv_sem=pan_recv.at[i, o],
            device_id=(row, me, other),
            device_id_type=MESH,
        )

    def shared(i, o):
        return pltpu.make_async_remote_copy(
            src_ref=arrived.at[other, i, behind(o)],
            dst_ref=arrived.at[other, i, behind(o)],
            send_sem=pan_send.at[i, o],
            recv_sem=pan_recv.at[i, o],
            device_id=(row, me, other),
            device_id_type=MESH,
        )

    def give_back(i, o):
        return pltpu.make_async_remote_copy(
            src_ref=outgoing.at[i, ahead(o)],
            dst_ref=home.at[i, me],
            send_sem=back_send.at[i, o],
            recv_sem=back_recv.at[i, o],
            device_id=(row, ahead(o), pan),
            device_id_type=MESH,
        )

    def got_back(i, o):
        return pltpu.make_async_remote_copy(
            src_ref=outgoing.at[i, behind(o)],
            dst_ref=home.at[i, behind(o)],
            send_sem=back_send.at[i, o],
            recv_sem=back_recv.at[i, o],
            device_id=(row, behind(o), pan),
            device_id_type=MESH,
        )


    def first_step(i, carry):
        load_first(i).wait()
        left = jnp.concatenate([first[i, q] for q in range(near1)], axis=1)
        step = 2 * half
        for n in range(slots * half // step):
            right = jnp.concatenate(
                [tm[near_smem[i, q], :, n * step : (n + 1) * step] for q in range(near1)], axis=0
            )
            piece = jnp.dot(left, right, preferred_element_type=jnp.float32).astype(jnp.bfloat16)
            product[2 * n] = piece[:, :half]
            product[2 * n + 1] = piece[:, half:]
        for o in list(range(1, C)) + [0]:
            d = ahead(o)
            for rank in range(CAP):
                slot = slot_of[d * CAP + rank]
                piece = product[jnp.maximum(slot, 0)]
                keep = (slot >= 0).astype(jnp.float32).astype(jnp.bfloat16)
                piece = piece if items == slots else piece * keep
                if o:
                    outgoing[i, d, rank] = piece
                else:
                    arrived[pan, i, me, rank] = piece
            if o:
                dispatch(i, o).start()
            else:
                share(i, 0).start()
        return carry

    lax.fori_loop(0, tiles, first_step, 0)

    for o in range(1, C):
        take_names(o).wait_recv()
    copy_names = pltpu.make_async_copy(names, names_all, local_sem.at[3])
    copy_names.start()
    copy_names.wait()
    for src in range(C):
        for rank in range(CAP):
            read = lambda s: names_all[src, 0, s]
            slot = ranked_slot(read, slots, blocks_here, me, rank)
            name = lax.rem(read(jnp.maximum(slot, 0)), jnp.int32(blocks_here))
            label_of[src * CAP + rank] = jnp.where(slot >= 0, name, jnp.int32(-1))
    for l in range(blocks_here):
        hits = jnp.int32(0)
        for t in range(items):
            hits = hits + (label_of[t] == l).astype(jnp.int32)
        present_of[l] = jnp.minimum(hits, 1)

    def index_step(k, carry):
        for l in range(blocks_here):
            found = jnp.int32(blocks_here * near2)
            for q in range(near2):
                found = jnp.where(near_second_smem[k, q] == l, k * near2 + q, found)
            second_index[k, l] = found
        return carry

    lax.fori_loop(0, blocks_here, index_step, 0)
    load_second.wait()

    def spread(line):
        return jnp.transpose(jnp.broadcast_to(line, (half, block)))

    def sums_out(i, oc, oh):
        mine = me * PAN + pan
        return pltpu.make_async_remote_copy(
            src_ref=row_sums.at[mine, i],
            dst_ref=row_sums.at[mine, i],
            send_sem=sum_send.at[i, oc * PAN + oh],
            recv_sem=sum_recv.at[i, oc * PAN + oh],
            device_id=(row, ahead(oc), other if oh else pan),
            device_id_type=MESH,
        )

    def sums_in(i, oc, oh):
        theirs = behind(oc) * PAN + (other if oh else pan)
        return pltpu.make_async_remote_copy(
            src_ref=row_sums.at[theirs, i],
            dst_ref=row_sums.at[theirs, i],
            send_sem=sum_send.at[i, oc * PAN + oh],
            recv_sem=sum_recv.at[i, oc * PAN + oh],
            device_id=(row, behind(oc), other if oh else pan),
            device_id_type=MESH,
        )

    peers = [(oc, oh) for oc in range(C) for oh in range(PAN) if oc or oh]

    def send_home(i):
        for o in range(1, C):
            give_back(i, o).start()

    def forward(i):
        for o in range(1, C):
            arrival(i, o).wait_recv()
            share(i, o).start()

    held = list(range(tiles))

    def release():
        if held:
            send_home(held.pop(0))

    def stage(i):
        at = pl.ds(pl.multiple_of(i * block, block), block)
        for o in range(1, C):
            dispatch(i, o).wait_send()
        for d in range(C):
            for rank in range(CAP):
                label = jnp.maximum(label_of[d * CAP + rank], 0)
                value = jnp.minimum(values[label, at, :], BF16_MAX).astype(jnp.bfloat16)
                outgoing[i, d, rank] = value

    def second_step(i, carry):
        for o in range(C):
            shared(i, o).wait_recv()
        at = pl.ds(pl.multiple_of(i * block, block), block)
        first_offset = spread(offset_first[:, at])
        labels = [jnp.maximum(label_of[t], 0) for t in range(items)]
        total = jnp.zeros((block, half), jnp.float32)
        for pair in range(blocks_here // 2):
            crossed = None
            for start in range(0, items, GROUP):
                group = range(start, min(start + GROUP, items))
                left = jnp.concatenate(
                    [arrived[p, i, t // CAP, t % CAP] for t in group for p in range(PAN)], axis=1
                )
                right = jnp.concatenate(
                    [
                        jnp.concatenate(
                            [second[second_index[labels[t], 2 * pair + e]] for e in range(2)],
                            axis=1,
                        )
                        for t in group
                    ],
                    axis=0,
                )
                part = jnp.dot(left, right, preferred_element_type=jnp.float32)
                crossed = part if crossed is None else crossed + part
            for e in range(2):
                l = 2 * pair + e
                here = crossed[:, e * half : (e + 1) * half]
                seen = present_of[l].astype(jnp.float32)
                value = seen * jnp.exp(here - first_offset - offset_second[l : l + 1, :])
                values[l, at, :] = value
                total = total + value
        row_sums[me * PAN + pan, i] = jnp.sum(jnp.transpose(total), axis=0, keepdims=True)
        for oc, oh in peers:
            sums_out(i, oc, oh).start()
        return carry

    def middle_step(i, carry):
        second_step(i, 0)
        forward(i + 1)
        stage(i)
        return carry

    forward(0)
    lax.fori_loop(0, tiles - 2, middle_step, 0)
    second_step(tiles - 2, 0)
    forward(tiles - 1)
    release()
    stage(tiles - 2)
    second_step(tiles - 1, 0)
    release()
    stage(tiles - 1)

    def keep(i):
        return pltpu.make_async_copy(outgoing.at[i, me], home.at[i, me], done_sem.at[i])

    for i in range(tiles):
        keep(i).start()
    for i in range(tiles):
        for oc, oh in peers:
            sums_in(i, oc, oh).wait_recv()
    width = float(slots * C * block)
    for i in range(tiles):
        part = slice(i * block, (i + 1) * block)
        totals = row_sums[0, i]
        for t in range(1, C * PAN):
            totals = totals + row_sums[t, i]
        scale_first_ref[:, part] = weight_first[:, part] * width / totals

    def col_step(i, sums):
        at = pl.ds(pl.multiple_of(i * block, block), block)
        scale = spread(scale_first_ref[:, at])
        return tuple(
            sums[l] + jnp.sum(values[l, at, :] * scale, axis=0, keepdims=True)
            for l in range(blocks_here)
        )

    sums = lax.fori_loop(
        0, tiles, col_step, tuple(jnp.zeros((1, half), jnp.float32) for _ in range(blocks_here))
    )
    for l in range(blocks_here):
        col_sums[row, l : l + 1, :] = sums[l]
        col_sums[row, blocks_here + l : blocks_here + l + 1, :] = jnp.full(
            (1, half), present_of[l].astype(jnp.float32) * float(rows_total), jnp.float32
        )

    def cols_out(o):
        return pltpu.make_async_remote_copy(
            src_ref=col_sums.at[row],
            dst_ref=col_sums.at[row],
            send_sem=col_send.at[o],
            recv_sem=col_recv.at[o],
            device_id=(row_ahead(o), me, pan),
            device_id_type=MESH,
        )

    def cols_in(o):
        return pltpu.make_async_remote_copy(
            src_ref=col_sums.at[row_behind(o)],
            dst_ref=col_sums.at[row_behind(o)],
            send_sem=col_send.at[o],
            recv_sem=col_recv.at[o],
            device_id=(row_behind(o), me, pan),
            device_id_type=MESH,
        )

    for o in range(1, R_AXIS):
        cols_out(o).start()
    release()
    for o in range(1, R_AXIS):
        cols_in(o).wait_recv()
    both = col_sums[0]
    for t in range(1, R_AXIS):
        both = both + col_sums[t]
    colsum, counts = both[:blocks_here], both[blocks_here:]
    scale_second = weight_second[...] * counts / jnp.where(counts > 0, colsum, 1.0)
    scale_second_ref[...] = scale_second
    scales[me] = scale_second

    def scale_out(o):
        return pltpu.make_async_remote_copy(
            src_ref=scales.at[me],
            dst_ref=scales.at[me],
            send_sem=scale_send.at[o],
            recv_sem=scale_recv.at[o],
            device_id=(row, ahead(o), pan),
            device_id_type=MESH,
        )

    def scale_in(o):
        return pltpu.make_async_remote_copy(
            src_ref=scales.at[behind(o)],
            dst_ref=scales.at[behind(o)],
            send_sem=scale_send.at[o],
            recv_sem=scale_recv.at[o],
            device_id=(row, behind(o), pan),
            device_id_type=MESH,
        )

    for o in range(1, C):
        scale_out(o).start()
    while held:
        release()
    for o in range(1, C):
        scale_in(o).wait_recv()

    scales_ref[...] = scales[...]
    for i in range(tiles):
        for o in range(1, C):
            got_back(i, o).wait_recv()

    def drain(i, carry):
        for o in range(C):
            share(i, o).wait_send()
        for oc, oh in peers:
            sums_out(i, oc, oh).wait_send()
        return carry

    lax.fori_loop(0, tiles, drain, 0)
    for i in range(tiles):
        for o in range(1, C):
            give_back(i, o).wait_send()
    for o in range(1, C):
        send_names(o).wait_send()
        scale_out(o).wait_send()
    for o in range(1, R_AXIS):
        cols_out(o).wait_send()
    for i in range(tiles):
        keep(i).wait()


def hand_out(
    blocks_here, names, home, first_in, second_in, scales, plan_out, first_out, second_out, wide, item_of
):
    _, _, _, rows, half = home.shape
    slots = plan_out.shape[1]

    def own_name(s):
        return names[0, s]

    @pl.when(pl.program_id(0) == 0)
    def _():
        for s in range(slots):
            panel = lax.div(own_name(s), jnp.int32(blocks_here))
            rank = jnp.int32(0)
            for t in range(s):
                rank = rank + (lax.div(own_name(t), jnp.int32(blocks_here)) == panel).astype(jnp.int32)
            item_of[0, s] = panel
            item_of[1, s] = jnp.minimum(rank, CAP - 1)
            item_of[2, s] = lax.rem(own_name(s), jnp.int32(blocks_here))

    scale = jnp.transpose(jnp.broadcast_to(first_in[...], (half, rows)))
    for s in range(slots):
        panel, rank, name = item_of[0, s], item_of[1, s], item_of[2, s]
        value = home[0, panel, rank].astype(jnp.float32) * scale
        value = value * scales[panel, pl.ds(name, 1), :]
        wide[pl.ds(s, rows, stride=slots), :] = value
    plan_out[...] = wide[...].reshape(rows, slots, half).astype(jnp.bfloat16)
    first_out[...] = first_in[...]
    second_out[...] = second_in[...]


def local(
    plan_values,
    plan_blocks,
    first_values,
    first_blocks,
    second_values,
    second_blocks,
    weight_first,
    weight_second,
    offset_first,
    offset_second,
):
    C, R_AXIS = lax.axis_size("col"), lax.axis_size("row")
    rows, slots, half = plan_values.shape
    tiles, near1, block, _ = first_values.shape
    blocks_here, near2 = second_blocks.shape
    dims = (C, R_AXIS, tiles, block, slots, half, blocks_here, near1, near2)
    bf16, f32, i32 = jnp.bfloat16, jnp.float32, jnp.int32
    vmem, smem = pltpu.VMEM, pltpu.SMEM
    dma = pltpu.SemaphoreType.DMA
    in_vmem, in_smem = pl.BlockSpec(memory_space=vmem), pl.BlockSpec(memory_space=smem)
    anywhere = pl.BlockSpec(memory_space=pl.ANY)
    home, scale_first, scale_second, scales = pl.pallas_call(
        functools.partial(kernel, dims),
        out_shape=(
            jax.ShapeDtypeStruct((tiles, C, CAP, block, half), bf16),
            jax.ShapeDtypeStruct((1, rows), f32),
            jax.ShapeDtypeStruct((blocks_here, half), f32),
            jax.ShapeDtypeStruct((C, blocks_here, half), f32),
        ),
        in_specs=[
            anywhere,
            in_smem,
            in_vmem,
            anywhere,
            in_smem,
            anywhere,
            in_smem,
            in_vmem,
            in_vmem,
            in_vmem,
            in_vmem,
        ],
        out_specs=(anywhere, in_vmem, in_vmem, in_vmem),
        scratch_shapes=[
            vmem((tiles, block, slots, half), bf16),
            vmem((block * slots, half), f32),
            vmem((tiles, block, slots * half), bf16),
            vmem((tiles, near1, block, block), bf16),
            vmem((blocks_here * near2 + 1, block, half), bf16),
            vmem((slots, block, half), bf16),
            vmem((tiles, C, CAP, block, half), bf16),
            vmem((PAN, tiles, C, CAP, block, half), bf16),
            vmem((blocks_here, rows, half), f32),
            vmem((C * PAN, tiles, 1, block), f32),
            vmem((R_AXIS, 2 * blocks_here, half), f32),
            vmem((C, blocks_here, half), f32),
            vmem((C, 8, 128), i32),
            smem((C, 8, 128), i32),
            smem((blocks_here, blocks_here), i32),
            smem((C * CAP,), i32),
            smem((C * CAP,), i32),
            smem((blocks_here,), i32),
            dma((4,)),
            dma((C,)),
            dma((C,)),
            dma((tiles, C)),
            dma((tiles, C)),
            dma((tiles, C)),
            dma((tiles, C)),
            dma((tiles, C)),
            dma((tiles, C)),
            dma((tiles, C * PAN)),
            dma((tiles, C * PAN)),
            dma((R_AXIS,)),
            dma((R_AXIS,)),
            dma((C,)),
            dma((C,)),
            dma((tiles,)),
            dma((tiles,)),
            dma((tiles,)),
        ],
        compiler_params=pltpu.CompilerParams(
            collective_id=0, has_side_effects=True, vmem_limit_bytes=60 * 1024 * 1024
        ),
        name="gromov_step",
    )(
        plan_values,
        plan_blocks,
        plan_blocks,
        first_values,
        first_blocks,
        second_values.reshape(blocks_here * near2, block, half),
        second_blocks,
        weight_first.reshape(1, rows),
        weight_second,
        offset_first.reshape(1, rows),
        offset_second,
    )
    step = block // 2
    out, scale_first, scale_second = pl.pallas_call(
        functools.partial(hand_out, blocks_here),
        out_shape=(
            jax.ShapeDtypeStruct((rows, slots, half), bf16),
            jax.ShapeDtypeStruct((1, rows), f32),
            jax.ShapeDtypeStruct((blocks_here, half), f32),
        ),
        grid=(2 * tiles,),
        in_specs=[
            in_smem,
            pl.BlockSpec((1, C, CAP, step, half), lambda i: (i // 2, 0, 0, i % 2, 0)),
            pl.BlockSpec((1, step), lambda i: (0, i)),
            pl.BlockSpec((blocks_here, half), lambda i: (0, 0)),
            pl.BlockSpec((C, blocks_here, half), lambda i: (0, 0, 0)),
        ],
        out_specs=(
            pl.BlockSpec((step, slots, half), lambda i: (i, 0, 0)),
            pl.BlockSpec((1, step), lambda i: (0, i)),
            pl.BlockSpec((blocks_here, half), lambda i: (0, 0)),
        ),
        scratch_shapes=[vmem((step * slots, half), f32), smem((3, slots), i32)],
        name="hand_out",
    )(plan_blocks, home, scale_first, scale_second, scales)
    return out, scale_first.reshape(rows), scale_second


def solution(mesh):
    return jax.shard_map(
        local,
        mesh=mesh,
        in_specs=(
            P("row", "col", "pan"),
            P("row", "col"),
            P("row", None, None, None),
            P("row", None),
            P("col", None, None, "pan"),
            P("col", None),
            P("row"),
            P("col", "pan"),
            P("row"),
            P("col", "pan"),
        ),
        out_specs=(P("row", "col", "pan"), P("row"), P("col", "pan")),
        check_vma=False,
    )
```

```python
import functools

import jax
import jax.numpy as jnp
from jax import lax
from jax.experimental import pallas as pl
from jax.experimental.pallas import tpu as pltpu
from jax.sharding import PartitionSpec as P

CAP = 2
PAN = 2
GROUP = 8
MESH = pl.DeviceIdType.MESH
BF16_MAX = float(jnp.finfo(jnp.bfloat16).max)


def ranked_slot(read, slots, blocks_here, panel, rank):
    seen, found = jnp.int32(0), jnp.int32(-1)
    for s in range(slots):
        match = (lax.div(read(s), jnp.int32(blocks_here)) == panel).astype(jnp.int32)
        hit = match * (seen == rank).astype(jnp.int32)
        found = jnp.where(hit > 0, jnp.int32(s), found)
        seen = seen + match
    return found


def kernel(
    dims,
    plan_hbm,
    names_smem,
    names_vmem,
    first_hbm,
    near_smem,
    second_hbm,
    near_second_smem,
    weight_first,
    weight_second,
    offset_first,
    offset_second,
    home,
    scale_first_ref,
    scale_second_ref,
    scales_ref,
    plan,
    tm,
    first,
    second,
    product,
    outgoing,
    arrived,
    values,
    row_sums,
    col_sums,
    scales,
    names,
    names_all,
    second_index,
    slot_of,
    label_of,
    present_of,
    local_sem,
    name_send,
    name_recv,
    out_send,
    out_recv,
    pan_send,
    pan_recv,
    back_send,
    back_recv,
    sum_send,
    sum_recv,
    col_send,
    col_recv,
    scale_send,
    scale_recv,
    plan_sem,
    first_sem,
    done_sem,
):
    C, R_AXIS, tiles, block, slots, half, blocks_here, near1, near2 = dims
    rows_total = tiles * block
    items = C * CAP
    row, me, pan = lax.axis_index("row"), lax.axis_index("col"), lax.axis_index("pan")
    other = 1 - pan

    def ahead(o):
        return lax.rem(me + o, C)

    def behind(o):
        return lax.rem(me - o + C, C)

    def row_ahead(o):
        return lax.rem(row + o, R_AXIS)

    def row_behind(o):
        return lax.rem(row - o + R_AXIS, R_AXIS)

    def load_plan(i):
        return pltpu.make_async_copy(
            plan_hbm.at[pl.ds(i * block, block)], plan.at[i], plan_sem.at[i]
        )

    def load_first(i):
        return pltpu.make_async_copy(first_hbm.at[i], first.at[i], first_sem.at[i])

    load_second = pltpu.make_async_copy(
        second_hbm, second.at[pl.ds(0, blocks_here * near2)], local_sem.at[2]
    )
    for i in range(tiles):
        load_plan(i).start()
    for i in range(tiles):
        load_first(i).start()

    barrier = pltpu.get_barrier_semaphore()
    for oc in range(C):
        for oh in range(PAN):
            if oc or oh:
                pl.semaphore_signal(
                    barrier,
                    inc=1,
                    device_id=(row, ahead(oc), other if oh else pan),
                    device_id_type=MESH,
                )
    for o in range(1, R_AXIS):
        pl.semaphore_signal(
            barrier, inc=1, device_id=(row_ahead(o), me, pan), device_id_type=MESH
        )

    names[me] = jnp.zeros((8, 128), jnp.int32)
    names[me, 0:1, 0:slots] = names_vmem[...]
    second[blocks_here * near2] = jnp.zeros((block, half), jnp.bfloat16)

    def own_name(s):
        return names_smem[0, s]

    for d in range(C):
        for rank in range(CAP):
            slot_of[d * CAP + rank] = ranked_slot(own_name, slots, blocks_here, d, rank)
    def relayout(i, carry):
        load_plan(i).wait()
        swapped = jnp.swapaxes(plan[i].astype(jnp.float32), 0, 1)
        for s in range(slots):
            tm[i, :, s * half : (s + 1) * half] = swapped[s].astype(jnp.bfloat16)
        return carry

    lax.fori_loop(0, tiles, relayout, 0)
    load_second.start()

    pl.semaphore_wait(barrier, C * PAN - 1 + R_AXIS - 1)

    def send_names(o):
        return pltpu.make_async_remote_copy(
            src_ref=names.at[me],
            dst_ref=names.at[me],
            send_sem=name_send.at[o],
            recv_sem=name_recv.at[o],
            device_id=(row, ahead(o), pan),
            device_id_type=MESH,
        )

    def take_names(o):
        src = behind(o)
        return pltpu.make_async_remote_copy(
            src_ref=names.at[src],
            dst_ref=names.at[src],
            send_sem=name_send.at[o],
            recv_sem=name_recv.at[o],
            device_id=(row, src, pan),
            device_id_type=MESH,
        )

    for o in range(1, C):
        send_names(o).start()

    def dispatch(i, o):
        return pltpu.make_async_remote_copy(
            src_ref=outgoing.at[i, ahead(o)],
            dst_ref=arrived.at[pan, i, me],
            send_sem=out_send.at[i, o],
            recv_sem=out_recv.at[i, o],
            device_id=(row, ahead(o), pan),
            device_id_type=MESH,
        )

    def arrival(i, o):
        return pltpu.make_async_remote_copy(
            src_ref=outgoing.at[i, behind(o)],
            dst_ref=arrived.at[pan, i, behind(o)],
            send_sem=out_send.at[i, o],
            recv_sem=out_recv.at[i, o],
            device_id=(row, behind(o), pan),
            device_id_type=MESH,
        )

    def share(i, o):
        return pltpu.make_async_remote_copy(
            src_ref=arrived.at[pan, i, behind(o)],
            dst_ref=arrived.at[pan, i, behind(o)],
            send_sem=pan_send.at[i, o],
            recv_sem=pan_recv.at[i, o],
            device_id=(row, me, other),
            device_id_type=MESH,
        )

    def shared(i, o):
        return pltpu.make_async_remote_copy(
            src_ref=arrived.at[other, i, behind(o)],
            dst_ref=arrived.at[other, i, behind(o)],
            send_sem=pan_send.at[i, o],
            recv_sem=pan_recv.at[i, o],
            device_id=(row, me, other),
            device_id_type=MESH,
        )

    def give_back(i, o):
        return pltpu.make_async_remote_copy(
            src_ref=outgoing.at[i, ahead(o)],
            dst_ref=home.at[i, me],
            send_sem=back_send.at[i, o],
            recv_sem=back_recv.at[i, o],
            device_id=(row, ahead(o), pan),
            device_id_type=MESH,
        )

    def got_back(i, o):
        return pltpu.make_async_remote_copy(
            src_ref=outgoing.at[i, behind(o)],
            dst_ref=home.at[i, behind(o)],
            send_sem=back_send.at[i, o],
            recv_sem=back_recv.at[i, o],
            device_id=(row, behind(o), pan),
            device_id_type=MESH,
        )


    def first_step(i, carry):
        load_first(i).wait()
        left = jnp.concatenate([first[i, q] for q in range(near1)], axis=1)
        step = 2 * half
        for n in range(slots * half // step):
            right = jnp.concatenate(
                [tm[near_smem[i, q], :, n * step : (n + 1) * step] for q in range(near1)], axis=0
            )
            piece = jnp.dot(left, right, preferred_element_type=jnp.float32).astype(jnp.bfloat16)
            product[2 * n] = piece[:, :half]
            product[2 * n + 1] = piece[:, half:]
        for o in list(range(1, C)) + [0]:
            d = ahead(o)
            for rank in range(CAP):
                slot = slot_of[d * CAP + rank]
                piece = product[jnp.maximum(slot, 0)]
                keep = (slot >= 0).astype(jnp.float32).astype(jnp.bfloat16)
                piece = piece if items == slots else piece * keep
                if o:
                    outgoing[i, d, rank] = piece
                else:
                    arrived[pan, i, me, rank] = piece
            if o:
                dispatch(i, o).start()
            else:
                share(i, 0).start()
        return carry

    lax.fori_loop(0, tiles, first_step, 0)

    for o in range(1, C):
        take_names(o).wait_recv()
    copy_names = pltpu.make_async_copy(names, names_all, local_sem.at[3])
    copy_names.start()
    copy_names.wait()
    for src in range(C):
        for rank in range(CAP):
            read = lambda s: names_all[src, 0, s]
            slot = ranked_slot(read, slots, blocks_here, me, rank)
            name = lax.rem(read(jnp.maximum(slot, 0)), jnp.int32(blocks_here))
            label_of[src * CAP + rank] = jnp.where(slot >= 0, name, jnp.int32(-1))
    for l in range(blocks_here):
        hits = jnp.int32(0)
        for t in range(items):
            hits = hits + (label_of[t] == l).astype(jnp.int32)
        present_of[l] = jnp.minimum(hits, 1)

    def index_step(k, carry):
        for l in range(blocks_here):
            found = jnp.int32(blocks_here * near2)
            for q in range(near2):
                found = jnp.where(near_second_smem[k, q] == l, k * near2 + q, found)
            second_index[k, l] = found
        return carry

    lax.fori_loop(0, blocks_here, index_step, 0)
    load_second.wait()

    def spread(line):
        return jnp.transpose(jnp.broadcast_to(line, (half, block)))

    def sums_out(i, oc, oh):
        mine = me * PAN + pan
        return pltpu.make_async_remote_copy(
            src_ref=row_sums.at[mine, i],
            dst_ref=row_sums.at[mine, i],
            send_sem=sum_send.at[i, oc * PAN + oh],
            recv_sem=sum_recv.at[i, oc * PAN + oh],
            device_id=(row, ahead(oc), other if oh else pan),
            device_id_type=MESH,
        )

    def sums_in(i, oc, oh):
        theirs = behind(oc) * PAN + (other if oh else pan)
        return pltpu.make_async_remote_copy(
            src_ref=row_sums.at[theirs, i],
            dst_ref=row_sums.at[theirs, i],
            send_sem=sum_send.at[i, oc * PAN + oh],
            recv_sem=sum_recv.at[i, oc * PAN + oh],
            device_id=(row, behind(oc), other if oh else pan),
            device_id_type=MESH,
        )

    peers = [(oc, oh) for oc in range(C) for oh in range(PAN) if oc or oh]

    def send_home(i):
        for o in range(1, C):
            give_back(i, o).start()

    def forward(i):
        for o in range(1, C):
            arrival(i, o).wait_recv()
            share(i, o).start()

    held = list(range(tiles))

    def release():
        if held:
            send_home(held.pop(0))

    def stage(i):
        at = pl.ds(pl.multiple_of(i * block, block), block)
        for o in range(1, C):
            dispatch(i, o).wait_send()
        for d in range(C):
            for rank in range(CAP):
                label = jnp.maximum(label_of[d * CAP + rank], 0)
                value = jnp.minimum(values[label, at, :], BF16_MAX).astype(jnp.bfloat16)
                outgoing[i, d, rank] = value

    def second_step(i, carry):
        for o in range(C):
            shared(i, o).wait_recv()
        at = pl.ds(pl.multiple_of(i * block, block), block)
        first_offset = spread(offset_first[:, at])
        labels = [jnp.maximum(label_of[t], 0) for t in range(items)]
        total = jnp.zeros((block, half), jnp.float32)
        for pair in range(blocks_here // 2):
            crossed = None
            for start in range(0, items, GROUP):
                group = range(start, min(start + GROUP, items))
                left = jnp.concatenate(
                    [arrived[p, i, t // CAP, t % CAP] for t in group for p in range(PAN)], axis=1
                )
                right = jnp.concatenate(
                    [
                        jnp.concatenate(
                            [second[second_index[labels[t], 2 * pair + e]] for e in range(2)],
                            axis=1,
                        )
                        for t in group
                    ],
                    axis=0,
                )
                part = jnp.dot(left, right, preferred_element_type=jnp.float32)
                crossed = part if crossed is None else crossed + part
            for e in range(2):
                l = 2 * pair + e
                here = crossed[:, e * half : (e + 1) * half]
                seen = present_of[l].astype(jnp.float32)
                value = seen * jnp.exp(here - first_offset - offset_second[l : l + 1, :])
                values[l, at, :] = value
                total = total + value
        row_sums[me * PAN + pan, i] = jnp.sum(jnp.transpose(total), axis=0, keepdims=True)
        for oc, oh in peers:
            sums_out(i, oc, oh).start()
        return carry

    def middle_step(i, carry):
        second_step(i, 0)
        forward(i + 1)
        stage(i)
        return carry

    forward(0)
    lax.fori_loop(0, tiles - 2, middle_step, 0)
    second_step(tiles - 2, 0)
    forward(tiles - 1)
    release()
    stage(tiles - 2)
    second_step(tiles - 1, 0)
    release()
    stage(tiles - 1)

    def keep(i):
        return pltpu.make_async_copy(outgoing.at[i, me], home.at[i, me], done_sem.at[i])

    for i in range(tiles):
        keep(i).start()
    for i in range(tiles):
        for oc, oh in peers:
            sums_in(i, oc, oh).wait_recv()
    width = float(slots * C * block)
    for i in range(tiles):
        part = slice(i * block, (i + 1) * block)
        totals = row_sums[0, i]
        for t in range(1, C * PAN):
            totals = totals + row_sums[t, i]
        scale_first_ref[:, part] = weight_first[:, part] * width / totals

    def col_step(i, sums):
        at = pl.ds(pl.multiple_of(i * block, block), block)
        scale = spread(scale_first_ref[:, at])
        return tuple(
            sums[l] + jnp.sum(values[l, at, :] * scale, axis=0, keepdims=True)
            for l in range(blocks_here)
        )

    sums = lax.fori_loop(
        0, tiles, col_step, tuple(jnp.zeros((1, half), jnp.float32) for _ in range(blocks_here))
    )
    for l in range(blocks_here):
        col_sums[row, l : l + 1, :] = sums[l]
        col_sums[row, blocks_here + l : blocks_here + l + 1, :] = jnp.full(
            (1, half), present_of[l].astype(jnp.float32) * float(rows_total), jnp.float32
        )

    def cols_out(o):
        return pltpu.make_async_remote_copy(
            src_ref=col_sums.at[row],
            dst_ref=col_sums.at[row],
            send_sem=col_send.at[o],
            recv_sem=col_recv.at[o],
            device_id=(row_ahead(o), me, pan),
            device_id_type=MESH,
        )

    def cols_in(o):
        return pltpu.make_async_remote_copy(
            src_ref=col_sums.at[row_behind(o)],
            dst_ref=col_sums.at[row_behind(o)],
            send_sem=col_send.at[o],
            recv_sem=col_recv.at[o],
            device_id=(row_behind(o), me, pan),
            device_id_type=MESH,
        )

    for o in range(1, R_AXIS):
        cols_out(o).start()
    release()
    for o in range(1, R_AXIS):
        cols_in(o).wait_recv()
    both = col_sums[0]
    for t in range(1, R_AXIS):
        both = both + col_sums[t]
    colsum, counts = both[:blocks_here], both[blocks_here:]
    scale_second = weight_second[...] * counts / jnp.where(counts > 0, colsum, 1.0)
    scale_second_ref[...] = scale_second
    scales[me] = scale_second

    def scale_out(o):
        return pltpu.make_async_remote_copy(
            src_ref=scales.at[me],
            dst_ref=scales.at[me],
            send_sem=scale_send.at[o],
            recv_sem=scale_recv.at[o],
            device_id=(row, ahead(o), pan),
            device_id_type=MESH,
        )

    def scale_in(o):
        return pltpu.make_async_remote_copy(
            src_ref=scales.at[behind(o)],
            dst_ref=scales.at[behind(o)],
            send_sem=scale_send.at[o],
            recv_sem=scale_recv.at[o],
            device_id=(row, behind(o), pan),
            device_id_type=MESH,
        )

    for o in range(1, C):
        scale_out(o).start()
    while held:
        release()
    for o in range(1, C):
        scale_in(o).wait_recv()

    scales_ref[...] = scales[...]
    for i in range(tiles):
        for o in range(1, C):
            got_back(i, o).wait_recv()

    def drain(i, carry):
        for o in range(C):
            share(i, o).wait_send()
        for oc, oh in peers:
            sums_out(i, oc, oh).wait_send()
        return carry

    lax.fori_loop(0, tiles, drain, 0)
    for i in range(tiles):
        for o in range(1, C):
            give_back(i, o).wait_send()
    for o in range(1, C):
        send_names(o).wait_send()
        scale_out(o).wait_send()
    for o in range(1, R_AXIS):
        cols_out(o).wait_send()
    for i in range(tiles):
        keep(i).wait()


def hand_out(
    blocks_here, names, home, first_in, second_in, scales, plan_out, first_out, second_out, item_of
):
    _, _, _, rows, half = home.shape
    slots = plan_out.shape[1]

    def own_name(s):
        return names[0, s]

    @pl.when(pl.program_id(0) == 0)
    def _():
        for s in range(slots):
            panel = lax.div(own_name(s), jnp.int32(blocks_here))
            rank = jnp.int32(0)
            for t in range(s):
                rank = rank + (lax.div(own_name(t), jnp.int32(blocks_here)) == panel).astype(jnp.int32)
            item_of[0, s] = panel
            item_of[1, s] = jnp.minimum(rank, CAP - 1)
            item_of[2, s] = lax.rem(own_name(s), jnp.int32(blocks_here))

    scale = jnp.transpose(jnp.broadcast_to(first_in[...], (half, rows)))
    pieces = []
    for s in range(slots):
        panel, rank, name = item_of[0, s], item_of[1, s], item_of[2, s]
        value = home[0, panel, rank].astype(jnp.float32) * scale
        pieces.append(value * scales[panel, pl.ds(name, 1), :])
    plan_out[...] = jnp.swapaxes(jnp.stack(pieces), 0, 1).astype(jnp.bfloat16)
    first_out[...] = first_in[...]
    second_out[...] = second_in[...]


def local(
    plan_values,
    plan_blocks,
    first_values,
    first_blocks,
    second_values,
    second_blocks,
    weight_first,
    weight_second,
    offset_first,
    offset_second,
):
    C, R_AXIS = lax.axis_size("col"), lax.axis_size("row")
    rows, slots, half = plan_values.shape
    tiles, near1, block, _ = first_values.shape
    blocks_here, near2 = second_blocks.shape
    dims = (C, R_AXIS, tiles, block, slots, half, blocks_here, near1, near2)
    bf16, f32, i32 = jnp.bfloat16, jnp.float32, jnp.int32
    vmem, smem = pltpu.VMEM, pltpu.SMEM
    dma = pltpu.SemaphoreType.DMA
    in_vmem, in_smem = pl.BlockSpec(memory_space=vmem), pl.BlockSpec(memory_space=smem)
    anywhere = pl.BlockSpec(memory_space=pl.ANY)
    home, scale_first, scale_second, scales = pl.pallas_call(
        functools.partial(kernel, dims),
        out_shape=(
            jax.ShapeDtypeStruct((tiles, C, CAP, block, half), bf16),
            jax.ShapeDtypeStruct((1, rows), f32),
            jax.ShapeDtypeStruct((blocks_here, half), f32),
            jax.ShapeDtypeStruct((C, blocks_here, half), f32),
        ),
        in_specs=[
            anywhere,
            in_smem,
            in_vmem,
            anywhere,
            in_smem,
            anywhere,
            in_smem,
            in_vmem,
            in_vmem,
            in_vmem,
            in_vmem,
        ],
        out_specs=(anywhere, in_vmem, in_vmem, in_vmem),
        scratch_shapes=[
            vmem((tiles, block, slots, half), bf16),
            vmem((tiles, block, slots * half), bf16),
            vmem((tiles, near1, block, block), bf16),
            vmem((blocks_here * near2 + 1, block, half), bf16),
            vmem((slots, block, half), bf16),
            vmem((tiles, C, CAP, block, half), bf16),
            vmem((PAN, tiles, C, CAP, block, half), bf16),
            vmem((blocks_here, rows, half), f32),
            vmem((C * PAN, tiles, 1, block), f32),
            vmem((R_AXIS, 2 * blocks_here, half), f32),
            vmem((C, blocks_here, half), f32),
            vmem((C, 8, 128), i32),
            smem((C, 8, 128), i32),
            smem((blocks_here, blocks_here), i32),
            smem((C * CAP,), i32),
            smem((C * CAP,), i32),
            smem((blocks_here,), i32),
            dma((4,)),
            dma((C,)),
            dma((C,)),
            dma((tiles, C)),
            dma((tiles, C)),
            dma((tiles, C)),
            dma((tiles, C)),
            dma((tiles, C)),
            dma((tiles, C)),
            dma((tiles, C * PAN)),
            dma((tiles, C * PAN)),
            dma((R_AXIS,)),
            dma((R_AXIS,)),
            dma((C,)),
            dma((C,)),
            dma((tiles,)),
            dma((tiles,)),
            dma((tiles,)),
        ],
        compiler_params=pltpu.CompilerParams(
            collective_id=0, has_side_effects=True, vmem_limit_bytes=60 * 1024 * 1024
        ),
        name="gromov_step",
    )(
        plan_values,
        plan_blocks,
        plan_blocks,
        first_values,
        first_blocks,
        second_values.reshape(blocks_here * near2, block, half),
        second_blocks,
        weight_first.reshape(1, rows),
        weight_second,
        offset_first.reshape(1, rows),
        offset_second,
    )
    step = block // 2
    out, scale_first, scale_second = pl.pallas_call(
        functools.partial(hand_out, blocks_here),
        out_shape=(
            jax.ShapeDtypeStruct((rows, slots, half), bf16),
            jax.ShapeDtypeStruct((1, rows), f32),
            jax.ShapeDtypeStruct((blocks_here, half), f32),
        ),
        grid=(2 * tiles,),
        in_specs=[
            in_smem,
            pl.BlockSpec((1, C, CAP, step, half), lambda i: (i // 2, 0, 0, i % 2, 0)),
            pl.BlockSpec((1, step), lambda i: (0, i)),
            pl.BlockSpec((blocks_here, half), lambda i: (0, 0)),
            pl.BlockSpec((C, blocks_here, half), lambda i: (0, 0, 0)),
        ],
        out_specs=(
            pl.BlockSpec((step, slots, half), lambda i: (i, 0, 0)),
            pl.BlockSpec((1, step), lambda i: (0, i)),
            pl.BlockSpec((blocks_here, half), lambda i: (0, 0)),
        ),
        scratch_shapes=[smem((3, slots), i32)],
        name="hand_out",
    )(plan_blocks, home, scale_first, scale_second, scales)
    return out, scale_first.reshape(rows), scale_second


def solution(mesh):
    return jax.shard_map(
        local,
        mesh=mesh,
        in_specs=(
            P("row", "col", "pan"),
            P("row", "col"),
            P("row", None, None, None),
            P("row", None),
            P("col", None, None, "pan"),
            P("col", None),
            P("row"),
            P("col", "pan"),
            P("row"),
            P("col", "pan"),
        ),
        out_specs=(P("row", "col", "pan"), P("row"), P("col", "pan")),
        check_vma=False,
    )
```
